128 devices in a mesh: ax: 8 (over x, core), az: 16 (over y, z).
Axes of the slice: x: 4, y: 4, z: 4, core: 2. Of those that a mesh axis runs over, the one named last changes fastest.
Arguments:
- state: float32 [5, 64, 128, 128], P(None, 'ax', 'az'), may hold values from -6 to 6
- surf_index: int32 [34816], P(('ax', 'az')), may hold values from 0 to 63
- surf_count: int32 [8, 16], P('ax', 'az'), may hold values from 1 to 272, as said below
- delay: int32 [34816, 2048], P(('ax', 'az')), may hold values from 0 to 510
- fraction: float32 [34816, 2048], P(('ax', 'az')), may hold values from 0 to 1
Outputs:
- signal: float32 [2048, 512], P(('ax', 'az'))
The draws below stay inside these ranges and needn't reach their ends.
Inputs may be any that keep to these rules, and one draw needn't show every extreme that they name: `surf_count`: devices in the first half of the axial index carry exactly 272 live slots; the others carry from 1 to 68.
All inputs are finite; a program needn't handle non-finite values.
Results may differ from the reference program's by a relative error of at most 0.0001.
Values sent between devices are 32-bit elements; how exact they have to be, the bound alone decides.
No kernel may reach another device: no remote copies, remote signals or barrier semaphores. Data moves between devices by JAX's collectives and lax.ppermute only.
A program may use at most 64 MiB of HBM per device.

```python
import jax
import jax.numpy as jnp
import numpy as np
from jax import lax

CX = 8
CY = 8
NZ = 128
SMAX = 272
NOBS = 2048
NT = 512
NX = 64
NY = 128
SLOTS = 34816
N_AX = 8
N_AZ = 16


def draw_surf_count(key, part):
    key = jax.random.fold_in(key, 7)
    lower = jax.random.randint(key, (N_AX, N_AZ), 1, SMAX // 4 + 1)
    band = jnp.arange(N_AX, dtype=jnp.int32)[:, None] < N_AX // 2
    return jnp.where(band, jnp.full((N_AX, N_AZ), SMAX, jnp.int32), lower).astype(jnp.int32)


def set_ends(entries, own_key, low, top_value):
    shape = entries.shape
    place = [jax.random.randint(jax.random.fold_in(own_key, axis), (), 0, shape[axis]) for axis in range(len(shape))]
    entries = entries.at[tuple(place)].set(low)
    longest = shape.index(max(shape))
    place[longest] = (place[longest] + 1) % shape[longest]
    return entries.at[tuple(place)].set(top_value)


def levels(key, shape, cuts, smallest, top_value):
    factor_of, own = 1.0, jax.random.fold_in(key, 6)
    for position, shards_of in cuts:
        steps = jnp.exp(jax.random.uniform(jax.random.fold_in(own, position), (shards_of,), jnp.float32, smallest / len(cuts), top_value / len(cuts)))
        factor_of = factor_of * jnp.repeat(steps, shape[position] // shards_of).reshape([-1 if axis == position else 1 for axis in range(len(shape))])
    return factor_of


def scatter_about(rng, extent, spread, most, shards=(), kind=jnp.bfloat16):
    values = jax.random.normal(rng, extent, jnp.float32) * spread
    if len(shards) > 0:
        values = levels(rng, extent, shards, -0.22, 0.18) * values
    return jnp.clip(values, min=-most, max=most).astype(kind)


def setup_inputs(seed: int = 0) -> dict:
    arg_keys = jax.random.split(jax.random.key(seed), 6)
    return {
        "state": scatter_about(arg_keys[0], (5, NX, NY, NZ), 1.0, 6.0, ((1, 8), (2, 16)), jnp.float32),
        "surf_index": set_ends(jax.random.randint(arg_keys[1], (SLOTS,), 0, CX * CY), jax.random.fold_in(arg_keys[1], 1), 0, (CX * CY) - 1).astype(jnp.int32),
        "surf_count": draw_surf_count(jax.random.fold_in(arg_keys[5], 71), 0),
        "delay": set_ends(jax.random.randint(arg_keys[3], (SLOTS, NOBS), 0, NT - 1), jax.random.fold_in(arg_keys[3], 1), 0, (NT - 1) - 1).astype(jnp.int32),
        "fraction": jnp.clip(1.0 * jax.random.uniform(arg_keys[4], (SLOTS, NOBS), jnp.float32) ** levels(arg_keys[4], (SLOTS, NOBS), ((0, 128),), -0.2, 0.2), 0.0, 1.0),
    }


MEAN_FLOW = 0.5
TIME_STEP = 0.05
AMPLITUDE = 0.05

def lobatto_matrix():
    points = np.array([-1.0, -1.0 / np.sqrt(5.0), 1.0 / np.sqrt(5.0), 1.0])
    table = np.zeros((4, 4))
    for i in range(4):
        for j in range(4):
            if i == j:
                table[i, j] = sum((1.0 / (points[i] - points[m]) for m in range(4) if m != i))
            else:
                a = np.prod([points[i] - points[m] for m in range(4) if m != i])
                b = np.prod([points[j] - points[m] for m in range(4) if m != j])
                table[i, j] = a / (b * (points[i] - points[j]))
    return table

def flux_axial(fields):
    density, vel_axial, vel_azim, vel_radial, pressure = (fields[0], fields[1], fields[2], fields[3], fields[4])
    return jnp.stack([MEAN_FLOW * density + vel_axial, MEAN_FLOW * vel_axial + pressure, MEAN_FLOW * vel_azim, MEAN_FLOW * vel_radial, MEAN_FLOW * pressure + vel_axial])

def flux_azimuthal(fields):
    zeros = jnp.zeros_like(fields[0])
    return jnp.stack([fields[2], zeros, fields[4], zeros, fields[2]])

def flux_radial(fields):
    zeros = jnp.zeros_like(fields[0])
    return jnp.stack([fields[3], zeros, zeros, fields[4], fields[3]])

def fr_derivative(padded, axis, flux_fn, speed):
    length = padded.shape[axis] - 2
    elements = length // 4
    inner = lax.slice_in_dim(padded, 1, length + 1, axis=axis)
    outer_left = lax.slice_in_dim(padded, 0, length, 4, axis)
    outer_right = lax.slice_in_dim(padded, 5, length + 2, 4, axis)
    first_node = lax.slice_in_dim(padded, 1, length + 1, 4, axis)
    last_node = lax.slice_in_dim(padded, 4, length + 2, 4, axis)
    flux_first = flux_fn(first_node)
    flux_last = flux_fn(last_node)
    common_left = 0.5 * (flux_fn(outer_left) + flux_first) - 0.5 * speed * (first_node - outer_left)
    common_right = 0.5 * (flux_last + flux_fn(outer_right)) - 0.5 * speed * (outer_right - last_node)
    shape = inner.shape
    split = shape[:axis] + (elements, 4) + shape[axis + 1:]
    blocks = flux_fn(inner).reshape(split)
    table = lobatto_matrix()
    bshape = [1] * len(split)
    bshape[axis + 1] = 4
    result = jnp.zeros(split, jnp.float32)
    for j in range(4):
        column = lax.slice_in_dim(blocks, j, j + 1, axis=axis + 1)
        result = result + jnp.asarray(table[:, j].reshape(bshape), jnp.float32) * column
    lift_right = jnp.asarray(np.array([0.0, 0.0, 0.0, 6.0]).reshape(bshape), jnp.float32)
    lift_left = jnp.asarray(np.array([6.0, 0.0, 0.0, 0.0]).reshape(bshape), jnp.float32)
    result = result + lift_right * jnp.expand_dims(common_right - flux_last, axis + 1)
    result = result - lift_left * jnp.expand_dims(common_left - flux_first, axis + 1)
    return result.reshape(shape)

def accumulate(total, values, delays, fracs):
    amplitude = AMPLITUDE * NT / (NT + delays.astype(jnp.float32))
    weighted = values[:, None] * amplitude
    index = jnp.arange(NOBS, dtype=jnp.int32)[None, :] * NT + delays
    total = total.at[index.reshape(-1)].add(((1.0 - fracs) * weighted).reshape(-1))
    total = total.at[(index + 1).reshape(-1)].add((fracs * weighted).reshape(-1))
    return total

def reference(state, surf_index, surf_count, delay, fraction):
    padded_x = jnp.pad(state, ((0, 0), (1, 1), (0, 0), (0, 0)))
    padded_y = jnp.concatenate([state[:, :, -1:], state, state[:, :, :1]], axis=2)
    padded_z = jnp.pad(state, ((0, 0), (0, 0), (0, 0), (1, 1)))
    change = fr_derivative(padded_x, 1, flux_axial, 1.5)
    change = change + fr_derivative(padded_y, 2, flux_azimuthal, 1.0)
    change = change + fr_derivative(padded_z, 3, flux_radial, 1.0)
    updated = state - TIME_STEP * change
    plane_index = 4 * (NZ // 8)
    plane = updated[4, :, :, plane_index] + updated[3, :, :, plane_index]
    slots = jnp.arange(N_AX * N_AZ * SMAX, dtype=jnp.int32)
    device = slots // SMAX
    row_axial = device // N_AZ
    col_azim = device % N_AZ
    point_x = row_axial * CX + surf_index // CY
    point_y = col_azim * CY + surf_index % CY
    source = plane[point_x, point_y]
    live = slots % SMAX < surf_count[row_axial, col_azim]
    source = jnp.where(live, source, jnp.zeros_like(source))

    def step_block(total, block):
        values, delays, fracs = block
        return (accumulate(total, values, delays, fracs), None)
    blocks = (source.reshape(N_AX * N_AZ, SMAX), delay.reshape(N_AX * N_AZ, SMAX, NOBS), fraction.reshape(N_AX * N_AZ, SMAX, NOBS))
    total, _ = lax.scan(step_block, jnp.zeros((NOBS * NT,), jnp.float32), blocks)
    return total.reshape(NOBS, NT)
```

```python
import jax
import jax.numpy as jnp
import numpy as np
from jax import lax
from jax.experimental import pallas as pl
from jax.experimental.pallas import tpu as pltpu
from jax.sharding import Mesh
from jax.sharding import PartitionSpec as P

SLOTS = 272
LANES = 640
RADIX = 15
ROWS = 36
BLOCK = 128
SAMPLES = 512
CHIP = ("x", "y", "z")


def lobatto_matrix():
    points = np.array([-1.0, -1.0 / np.sqrt(5.0), 1.0 / np.sqrt(5.0), 1.0])
    table = np.zeros((4, 4))
    for i in range(4):
        for j in range(4):
            if i == j:
                table[i, j] = sum((1.0 / (points[i] - points[m]) for m in range(4) if m != i))
            else:
                a = np.prod([points[i] - points[m] for m in range(4) if m != i])
                b = np.prod([points[j] - points[m] for m in range(4) if m != j])
                table[i, j] = a / (b * (points[i] - points[j]))
    return table


def line_derivative(flux, value, speed):
    table = lobatto_matrix()
    out = []
    for start in (1, 5):
        def common(low):
            return 0.5 * (flux[low] + flux[low + 1]) - 0.5 * speed * (value[low + 1] - value[low])
        rows = [
            sum(np.float32(table[i, j]) * flux[start + j] for j in range(4)) for i in range(4)
        ]
        rows[3] = rows[3] + 6.0 * (common(start + 3) - flux[start + 3])
        rows[0] = rows[0] - 6.0 * (common(start - 1) - flux[start])
        out += rows
    return jnp.stack(out)


def surface_plane(state):
    at = 4 * (state.shape[3] // 8)
    near = state[3, :, :, at - 1 : at + 4] + state[4, :, :, at - 1 : at + 4]
    value = near[:, :, 1]
    along = 0.5 * value + state[1, :, :, at]
    across = state[2, :, :, at]

    def ends(flux, axes, size, wrap):
        up = [(i, (i + 1) % size) for i in range(size if wrap else size - 1)]
        down = [(j, i) for i, j in up]
        both = jnp.stack([flux, value], axis=0)
        before = lax.ppermute(both[:, 7], axes, up)
        after = lax.ppermute(both[:, 0], axes, down)
        return jnp.concatenate([before[:, None], both, after[:, None]], axis=1)

    both = ends(along, ("x", "core"), lax.axis_size("x") * lax.axis_size("core"), False)
    change = line_derivative(both[0], both[1], 1.5)
    value_t = value
    value = value.T
    both = ends(across.T, ("y", "z"), lax.axis_size("y") * lax.axis_size("z"), True)
    change = change + line_derivative(both[0], both[1], 1.0).T
    value = value_t
    table = lobatto_matrix()
    radial = sum(np.float32(table[0, j]) * near[:, :, 1 + j] for j in range(4))
    common = 0.5 * (near[:, :, 0] + value) - 0.5 * (value - near[:, :, 0])
    change = change + (radial - 6.0 * (common - value))
    return value - 0.05 * change


def slot_source(state, surf_index, surf_count):
    plane = surface_plane(state).reshape(-1)
    points = jnp.arange(64, dtype=jnp.int32)
    source = jnp.sum(jnp.where(surf_index[None, :] == points[:, None], plane[:, None], 0.0), axis=0)
    live = jnp.arange(SLOTS, dtype=jnp.int32) < surf_count[0, 0]
    return jnp.where(live, source, 0.0)


def bins_kernel(core_ref, src_ref, da_ref, fa_ref, db_ref, fb_ref, out_ref, d_t, f_t, hi_s, *, unroll=2):
    def flip(a_ref, b_ref, dst, cast):
        for n, (r, base) in enumerate(((a_ref, 0), (a_ref, 128), (b_ref, 0), (b_ref, 128))):
            dst[:, n * 128:(n + 1) * 128] = cast(r[base:base + 128, :]).T
        rest = jnp.concatenate([cast(a_ref[256:272, :]), cast(b_ref[256:272, :]), jnp.zeros((96, 128), jnp.float32)], axis=0)
        dst[:, 512:640] = rest.T
    flip(da_ref, db_ref, d_t, lambda v: v.astype(jnp.float32))
    flip(fa_ref, fb_ref, f_t, lambda v: v)
    src = src_ref[...]
    row16 = lax.broadcasted_iota(jnp.int32, (16, LANES), 0)
    half = (row16 >= 8).astype(jnp.float32)
    count_lo = row16.astype(jnp.float32).astype(jnp.bfloat16)
    count_up = (row16 + 16).astype(jnp.float32).astype(jnp.bfloat16)
    one = jnp.ones((16, LANES), jnp.bfloat16)
    zero = jnp.zeros((16, LANES), jnp.bfloat16)
    lane = lax.broadcasted_iota(jnp.int32, (32, 128), 1) & 7
    lane8 = lax.broadcasted_iota(jnp.int32, (8, 128), 1) & 7
    diag8 = lane8 == lax.broadcasted_iota(jnp.int32, (8, 128), 0)

    def group(g, slot):
        rows = pl.ds(pl.multiple_of(g * 8, 8), 8)
        k = d_t[rows, :]
        f = f_t[rows, :]
        c = src * (25.6 / (512.0 + k))
        up = f * c
        low = c - up
        hi = jnp.floor((k + 0.5) * (1.0 / 15.0))
        lo = k - 15.0 * hi
        hi_s[slot] = hi
        twice = lambda v: jnp.concatenate([v, v], axis=0)
        lo2 = (twice(lo) - half).astype(jnp.bfloat16)
        hi2 = (twice(hi) - half).astype(jnp.bfloat16)
        def parts(v):
            top = v.astype(jnp.bfloat16)
            rest = (v - top.astype(jnp.float32))
            return twice(v).astype(jnp.bfloat16), twice(rest).astype(jnp.bfloat16)
        low_a, low_b = parts(low)
        up_a, up_b = parts(up)
        wa, wb = [], []
        for j in range(0, 16, 2):
            at = lo2 == jnp.bfloat16(j)
            before = lo2 == jnp.bfloat16(j - 1)
            wa.append(jnp.where(at, low_a, jnp.where(before, up_a, zero)))
            wb.append(jnp.where(at, low_b, jnp.where(before, up_b, zero)))
        w = jnp.concatenate(wa + wb, axis=0)
        h = []
        for o in range(8):
            row = jnp.broadcast_to(hi_s[slot, o:o + 1, :], (16, LANES)).astype(jnp.bfloat16)
            h.append(jnp.where(row == count_lo, one, zero))
            h.append(jnp.where(row == count_up, one, zero))
        h.append(jnp.where(hi2 == jnp.bfloat16(32), one, zero))
        h.append(jnp.where(hi2 == jnp.bfloat16(34), one, zero))
        h = jnp.concatenate(h, axis=0)
        r = lax.dot_general(h, w, (((1,), (1,)), ((), ())), preferred_element_type=jnp.float32)
        r = r[:, :128] + r[:, 128:]
        main = r[0:32]
        for o in range(1, 8):
            main = jnp.where(lane == o, r[32 * o:32 * o + 32], main)
        extra = [jnp.sum(jnp.where(diag8, r[256 + 8 * e:264 + 8 * e], 0.0), axis=0, keepdims=True) for e in range(4)]
        return jnp.concatenate([main] + extra, axis=0)

    def pair(p, _):
        two = [group(2 * p + t, t) for t in range(2)]
        out_ref[p] = jnp.concatenate(two, axis=0)
        return 0
    lax.fori_loop(0, BLOCK // 16, pair, 0, unroll=False)

def bins(core, src, delay, frac, delay_b, frac_b, first, blocks):
    own = lambda n, c: (0, ((n + first) // 2) * 4 + c[0] * 2 + (n + first) % 2)
    sib = lambda n, c: (0, n + first)
    spec = pl.BlockSpec((SLOTS, BLOCK), own)
    spec_b = pl.BlockSpec((SLOTS, BLOCK), sib)
    return pl.pallas_call(
        bins_kernel,
        grid_spec=pltpu.PrefetchScalarGridSpec(
            num_scalar_prefetch=1, grid=(blocks,),
            in_specs=[pl.BlockSpec((1, LANES), lambda n, c: (0, 0)), spec, spec, spec_b, spec_b],
            out_specs=pl.BlockSpec((8, 2 * ROWS, 128), lambda n, c: (n, 0, 0)),
            scratch_shapes=[pltpu.VMEM((BLOCK, LANES), jnp.float32), pltpu.VMEM((BLOCK, LANES), jnp.float32), pltpu.VMEM((2, 8, LANES), jnp.float32)],
        ),
        out_shape=jax.ShapeDtypeStruct((8 * blocks, 2 * ROWS, 128), jnp.float32),
        compiler_params=pltpu.CompilerParams(vmem_limit_bytes=48 * 1024 * 1024),
        name="bins",
    )(core, src, delay, frac, delay_b, frac_b)


def local(state, surf_index, surf_count, delay, fraction):
    core = lax.axis_index("core")
    swap = [(0, 1), (1, 0)]

    def other_half(rows):
        halves = rows.reshape(SLOTS, 4, 2, 256)
        return lax.dynamic_index_in_dim(halves, 1 - core, 2, keepdims=False).reshape(SLOTS, 1024)

    delay_b = lax.ppermute(other_half(delay), "core", swap)
    fraction_b = lax.ppermute(other_half(fraction), "core", swap)
    source = slot_source(state, surf_index, surf_count)
    source_b = lax.ppermute(source, "core", swap)
    source = jnp.concatenate(
        [source[:256], source_b[:256], source[256:], source_b[256:], jnp.zeros((96,), jnp.float32)]
    )
    sums = bins(core.reshape(1), source[None, :], delay, fraction, delay_b, fraction_b, 0, 8)
    parts = lax.all_to_all(sums, CHIP, 0, 0, tiled=True)
    total = jnp.sum(parts, axis=0)
    total = total.reshape(2, ROWS, 16, 8).transpose(0, 3, 1, 2).reshape(16, ROWS, 16)
    carry = jnp.pad(total[:, :34, 15:], ((0, 0), (1, 0), (0, 14)))
    return (total[:, :35, :RADIX] + carry).reshape(16, 35 * RADIX)[:, :SAMPLES]


def solution(mesh):
    fine = Mesh(mesh.devices.reshape(4, 2, 4, 4), ("x", "core", "y", "z"))
    ax, az = ("x", "core"), ("y", "z")
    placed = (
        P(None, ax, az, None),
        P(ax + az),
        P(ax, az),
        P(ax + az, None),
        P(ax + az, None),
    )
    return jax.shard_map(
        local, mesh=fine, in_specs=placed, out_specs=P(ax + az, None), check_vma=False
    )
```

```python
import jax
import jax.numpy as jnp
import numpy as np
from jax import lax
from jax.experimental import pallas as pl
from jax.experimental.pallas import tpu as pltpu
from jax.sharding import Mesh
from jax.sharding import PartitionSpec as P

SLOTS = 272
LANES = 640
RADIX = 15
ROWS = 36
BLOCK = 128
SAMPLES = 512
CHIP = ("x", "y", "z")
AXIAL = ("x", "core")
AZIMUTHAL = ("y", "z")
MEAN_FLOW = 0.5
TIME_STEP = 0.05


def lobatto_matrix():
    points = np.array([-1.0, -1.0 / np.sqrt(5.0), 1.0 / np.sqrt(5.0), 1.0])
    table = np.zeros((4, 4))
    for i in range(4):
        for j in range(4):
            if i == j:
                table[i, j] = sum((1.0 / (points[i] - points[m]) for m in range(4) if m != i))
            else:
                a = np.prod([points[i] - points[m] for m in range(4) if m != i])
                b = np.prod([points[j] - points[m] for m in range(4) if m != j])
                table[i, j] = a / (b * (points[i] - points[j]))
    return table


def line_operators():
    table = lobatto_matrix()

    def derivative(flux, value, speed):
        out = np.zeros((8,) + flux.shape[1:])
        for start in (1, 5):
            def common(low):
                mean = 0.5 * (flux[low] + flux[low + 1])
                return mean - 0.5 * speed * (value[low + 1] - value[low])
            for i in range(4):
                out[start - 1 + i] = sum(table[i, j] * flux[start + j] for j in range(4))
            out[start + 2] += 6.0 * (common(start + 3) - flux[start + 3])
            out[start - 1] -= 6.0 * (common(start - 1) - flux[start])
        return out

    def maps(along_axial):
        result = []
        for place in range(3):
            unit = np.zeros((24, 8, 128))
            for point in range(64):
                line, other = (point // 8, point % 8) if along_axial else (point % 8, point // 8)
                unit[place * 8 + line, other, point] = 1.0
            value = unit[7:17]
            speed_of = np.zeros((24, 8, 128))
            for point in range(64):
                line, other = (point // 8, point % 8) if along_axial else (point % 8, point // 8)
                speed_of[place * 8 + line, other, 64 + point] = 1.0
            velocity = speed_of[7:17]
            if along_axial:
                change = derivative(MEAN_FLOW * value + velocity, value, 1.5)
            else:
                change = np.swapaxes(derivative(velocity, value, 1.0), 0, 1)
            result.append(-TIME_STEP * change.reshape(64, 128).T)
        return result

    before_x, own_x, after_x = maps(True)
    before_y, own_y, after_y = maps(False)
    eye = np.eye(64)
    own_x[:64] += eye
    own_x[:64] -= TIME_STEP * (table[0, 0] - 6.0 * (0.5 - 0.5 - 1.0)) * eye
    low = -TIME_STEP * -6.0 * (0.5 + 0.5) * eye
    near_a = np.concatenate([low, -TIME_STEP * table[0, 1] * eye])
    near_b = np.concatenate([-TIME_STEP * table[0, 2] * eye, -TIME_STEP * table[0, 3] * eye])
    every = [own_x, own_y, near_a, near_b, before_x, after_x, before_y, after_y]
    return np.concatenate(every).astype(np.float32)


def tile_kernel(state_ref, tile_ref):
    at = 4 * (state_ref.shape[2] // 8)
    pick = lax.broadcasted_iota(jnp.int32, (8, 128), 1) == (
        lax.broadcasted_iota(jnp.int32, (8, 128), 0) + (at - 1)
    )
    pick = pick.astype(jnp.float32)

    def points(field):
        return lax.dot_general(
            pick, field, (((1,), (1,)), ((), ())),
            precision=lax.Precision.HIGHEST, preferred_element_type=jnp.float32,
        )

    value = points(state_ref[3] + state_ref[4])
    axial = points(state_ref[1])
    azimuthal = points(state_ref[2])
    rows = [
        jnp.concatenate([value[1:2], axial[1:2]], axis=1),
        jnp.concatenate([value[1:2], azimuthal[1:2]], axis=1),
        jnp.concatenate([value[0:1], value[2:3]], axis=1),
        jnp.concatenate([value[3:4], value[4:5]], axis=1),
        jnp.zeros((4, 128), jnp.float32),
    ]
    tile_ref[...] = jnp.concatenate(rows, axis=0)


def source_kernel(map_ref, own_ref, bx_ref, ax_ref, by_ref, ay_ref, index_ref, count_ref, source_ref):
    rows = [own_ref[0:1], own_ref[1:2], own_ref[2:3], own_ref[3:4],
            bx_ref[0:1], ax_ref[0:1], by_ref[1:2], ay_ref[1:2]]
    exact = dict(precision=lax.Precision.HIGHEST, preferred_element_type=jnp.float32)
    plane = jnp.dot(jnp.concatenate(rows, axis=1), map_ref[...], **exact)
    points = lax.broadcasted_iota(jnp.int32, (64, SLOTS), 0)
    hit = (index_ref[...] == points).astype(jnp.float32)
    source = jnp.dot(plane, hit, **exact)
    live = lax.broadcasted_iota(jnp.int32, (1, SLOTS), 1) < count_ref[0, 0]
    source_ref[...] = jnp.where(live, source, 0.0)


def slot_source(state, surf_index, surf_count):
    vmem = pl.BlockSpec(memory_space=pltpu.VMEM)
    tile = pl.pallas_call(
        tile_kernel,
        in_specs=[vmem],
        out_specs=vmem,
        out_shape=jax.ShapeDtypeStruct((8, 128), jnp.float32),
        name="tile",
    )(state.reshape(5, 64, state.shape[3]))

    def around(axes, size, wrap):
        up = [(i, (i + 1) % size) for i in range(size if wrap else size - 1)]
        down = [(j, i) for i, j in up]
        return lax.ppermute(tile, axes, up), lax.ppermute(tile, axes, down)

    before_x, after_x = around(AXIAL, lax.axis_size(AXIAL), False)
    before_y, after_y = around(AZIMUTHAL, lax.axis_size(AZIMUTHAL), True)
    return pl.pallas_call(
        source_kernel,
        in_specs=[vmem] * 7 + [pl.BlockSpec(memory_space=pltpu.SMEM)],
        out_specs=vmem,
        out_shape=jax.ShapeDtypeStruct((1, SLOTS), jnp.float32),
        name="source",
    )(
        jnp.asarray(line_operators()), tile, before_x, after_x, before_y, after_y,
        surf_index.reshape(1, SLOTS), surf_count,
    )


def half_kernel(core_ref, delay_ref, fraction_ref, delay_out, fraction_out):
    delay_out[...] = delay_ref[...]
    fraction_out[...] = fraction_ref[...]


def other_half(core, delay, fraction):
    width = delay.shape[1] // 8
    taken = pl.BlockSpec((SLOTS, width), lambda n, c: (0, 2 * n + 1 - c[0]))
    given = pl.BlockSpec((SLOTS, width), lambda n, c: (0, n))
    return pl.pallas_call(
        half_kernel,
        grid_spec=pltpu.PrefetchScalarGridSpec(
            num_scalar_prefetch=1, grid=(4,), in_specs=[taken] * 2, out_specs=[given] * 2
        ),
        out_shape=[
            jax.ShapeDtypeStruct((SLOTS, 4 * width), jnp.int32),
            jax.ShapeDtypeStruct((SLOTS, 4 * width), jnp.float32),
        ],
        name="other_half",
    )(core, delay, fraction)


def bins_kernel(core_ref, src_ref, src_b_ref, da_ref, fa_ref, db_ref, fb_ref, out_ref, d_t, f_t, hi_s, *, unroll=2):
    def flip(a_ref, b_ref, dst, cast):
        for n, (r, base) in enumerate(((a_ref, 0), (a_ref, 128), (b_ref, 0), (b_ref, 128))):
            dst[:, n * 128:(n + 1) * 128] = cast(r[base:base + 128, :]).T
        rest = jnp.concatenate([cast(a_ref[256:272, :]), cast(b_ref[256:272, :]), jnp.zeros((96, 128), jnp.float32)], axis=0)
        dst[:, 512:640] = rest.T
    flip(da_ref, db_ref, d_t, lambda v: v.astype(jnp.float32))
    flip(fa_ref, fb_ref, f_t, lambda v: v)
    src = jnp.concatenate(
        [src_ref[:, :256], src_b_ref[:, :256], src_ref[:, 256:], src_b_ref[:, 256:],
         jnp.zeros((1, 96), jnp.float32)], axis=1)
    row16 = lax.broadcasted_iota(jnp.int32, (16, LANES), 0)
    half = (row16 >= 8).astype(jnp.float32)
    count_lo = row16.astype(jnp.float32).astype(jnp.bfloat16)
    count_up = (row16 + 16).astype(jnp.float32).astype(jnp.bfloat16)
    one = jnp.ones((16, LANES), jnp.bfloat16)
    zero = jnp.zeros((16, LANES), jnp.bfloat16)
    lane = lax.broadcasted_iota(jnp.int32, (32, 128), 1) & 7
    lane8 = lax.broadcasted_iota(jnp.int32, (8, 128), 1) & 7
    diag8 = lane8 == lax.broadcasted_iota(jnp.int32, (8, 128), 0)

    def group(g, slot):
        rows = pl.ds(pl.multiple_of(g * 8, 8), 8)
        k = d_t[rows, :]
        f = f_t[rows, :]
        c = src * (25.6 / (512.0 + k))
        up = f * c
        low = c - up
        hi = jnp.floor((k + 0.5) * (1.0 / 15.0))
        lo = k - 15.0 * hi
        hi_s[slot] = hi
        twice = lambda v: jnp.concatenate([v, v], axis=0)
        lo2 = (twice(lo) - half).astype(jnp.bfloat16)
        hi2 = (twice(hi) - half).astype(jnp.bfloat16)
        def parts(v):
            top = v.astype(jnp.bfloat16)
            rest = (v - top.astype(jnp.float32))
            return twice(v).astype(jnp.bfloat16), twice(rest).astype(jnp.bfloat16)
        low_a, low_b = parts(low)
        up_a, up_b = parts(up)
        wa, wb = [], []
        for j in range(0, 16, 2):
            at = lo2 == jnp.bfloat16(j)
            before = lo2 == jnp.bfloat16(j - 1)
            wa.append(jnp.where(at, low_a, jnp.where(before, up_a, zero)))
            wb.append(jnp.where(at, low_b, jnp.where(before, up_b, zero)))
        w = jnp.concatenate(wa + wb, axis=0)
        h = []
        for o in range(8):
            row = jnp.broadcast_to(hi_s[slot, o:o + 1, :], (16, LANES)).astype(jnp.bfloat16)
            h.append(jnp.where(row == count_lo, one, zero))
            h.append(jnp.where(row == count_up, one, zero))
        h.append(jnp.where(hi2 == jnp.bfloat16(32), one, zero))
        h.append(jnp.where(hi2 == jnp.bfloat16(34), one, zero))
        h = jnp.concatenate(h, axis=0)
        r = lax.dot_general(h, w, (((1,), (1,)), ((), ())), preferred_element_type=jnp.float32)
        r = r[:, :128] + r[:, 128:]
        main = r[0:32]
        for o in range(1, 8):
            main = jnp.where(lane == o, r[32 * o:32 * o + 32], main)
        extra = [jnp.sum(jnp.where(diag8, r[256 + 8 * e:264 + 8 * e], 0.0), axis=0, keepdims=True) for e in range(4)]
        return jnp.concatenate([main] + extra, axis=0)

    def pair(p, _):
        two = [group(2 * p + t, t) for t in range(2)]
        out_ref[p] = jnp.concatenate(two, axis=0)
        return 0
    lax.fori_loop(0, BLOCK // 16, pair, 0, unroll=False)

def bins(core, src, src_b, delay, frac, delay_b, frac_b, first, blocks):
    own = lambda n, c: (0, ((n + first) // 2) * 4 + c[0] * 2 + (n + first) % 2)
    sib = lambda n, c: (0, n + first)
    spec = pl.BlockSpec((SLOTS, BLOCK), own)
    spec_b = pl.BlockSpec((SLOTS, BLOCK), sib)
    return pl.pallas_call(
        bins_kernel,
        grid_spec=pltpu.PrefetchScalarGridSpec(
            num_scalar_prefetch=1, grid=(blocks,),
            in_specs=[pl.BlockSpec((1, SLOTS), lambda n, c: (0, 0))] * 2 + [spec, spec, spec_b, spec_b],
            out_specs=pl.BlockSpec((8, 2 * ROWS, 128), lambda n, c: (n, 0, 0)),
            scratch_shapes=[pltpu.VMEM((BLOCK, LANES), jnp.float32), pltpu.VMEM((BLOCK, LANES), jnp.float32), pltpu.VMEM((2, 8, LANES), jnp.float32)],
        ),
        out_shape=jax.ShapeDtypeStruct((8 * blocks, 2 * ROWS, 128), jnp.float32),
        compiler_params=pltpu.CompilerParams(vmem_limit_bytes=48 * 1024 * 1024),
        name="bins",
    )(core, src, src_b, delay, frac, delay_b, frac_b)


def local(state, surf_index, surf_count, delay, fraction):
    core = lax.axis_index("core").reshape(1)
    swap = [(0, 1), (1, 0)]
    delay_b, fraction_b = other_half(core, delay, fraction)
    delay_b = lax.ppermute(delay_b, "core", swap)
    fraction_b = lax.ppermute(fraction_b, "core", swap)
    source = slot_source(state, surf_index, surf_count)
    source_b = lax.ppermute(source, "core", swap)
    sums = bins(core, source, source_b, delay, fraction, delay_b, fraction_b, 0, 8)
    parts = lax.all_to_all(sums, CHIP, 0, 0, tiled=True)
    total = jnp.sum(parts, axis=0)
    total = total.reshape(2, ROWS, 16, 8).transpose(0, 3, 1, 2).reshape(16, ROWS, 16)
    carry = jnp.pad(total[:, :34, 15:], ((0, 0), (1, 0), (0, 14)))
    return (total[:, :35, :RADIX] + carry).reshape(16, 35 * RADIX)[:, :SAMPLES]


def solution(mesh):
    fine = Mesh(mesh.devices.reshape(4, 2, 4, 4), ("x", "core", "y", "z"))
    ax, az = ("x", "core"), ("y", "z")
    placed = (
        P(None, ax, az, None),
        P(ax + az),
        P(ax, az),
        P(ax + az, None),
        P(ax + az, None),
    )
    return jax.shard_map(
        local, mesh=fine, in_specs=placed, out_specs=P(ax + az, None), check_vma=False
    )
```

```python
import jax
import jax.numpy as jnp
import numpy as np
from jax import lax
from jax.experimental import pallas as pl
from jax.experimental.pallas import tpu as pltpu
from jax.sharding import Mesh
from jax.sharding import PartitionSpec as P

SLOTS = 272
LANES = 640
RADIX = 15
ROWS = 36
BLOCK = 128
SAMPLES = 512
CHIP = ("x", "y", "z")
AXIAL = ("x", "core")
AZIMUTHAL = ("y", "z")
MEAN_FLOW = 0.5
TIME_STEP = 0.05


def lobatto_matrix():
    points = np.array([-1.0, -1.0 / np.sqrt(5.0), 1.0 / np.sqrt(5.0), 1.0])
    table = np.zeros((4, 4))
    for i in range(4):
        for j in range(4):
            if i == j:
                table[i, j] = sum((1.0 / (points[i] - points[m]) for m in range(4) if m != i))
            else:
                a = np.prod([points[i] - points[m] for m in range(4) if m != i])
                b = np.prod([points[j] - points[m] for m in range(4) if m != j])
                table[i, j] = a / (b * (points[i] - points[j]))
    return table


def line_operators():
    table = lobatto_matrix()

    def derivative(flux, value, speed):
        out = np.zeros((8,) + flux.shape[1:])
        for start in (1, 5):
            def common(low):
                mean = 0.5 * (flux[low] + flux[low + 1])
                return mean - 0.5 * speed * (value[low + 1] - value[low])
            for i in range(4):
                out[start - 1 + i] = sum(table[i, j] * flux[start + j] for j in range(4))
            out[start + 2] += 6.0 * (common(start + 3) - flux[start + 3])
            out[start - 1] -= 6.0 * (common(start - 1) - flux[start])
        return out

    def maps(along_axial):
        result = []
        for place in range(3):
            unit = np.zeros((24, 8, 128))
            for point in range(64):
                line, other = (point // 8, point % 8) if along_axial else (point % 8, point // 8)
                unit[place * 8 + line, other, point] = 1.0
            value = unit[7:17]
            speed_of = np.zeros((24, 8, 128))
            for point in range(64):
                line, other = (point // 8, point % 8) if along_axial else (point % 8, point // 8)
                speed_of[place * 8 + line, other, 64 + point] = 1.0
            velocity = speed_of[7:17]
            if along_axial:
                change = derivative(MEAN_FLOW * value + velocity, value, 1.5)
            else:
                change = np.swapaxes(derivative(velocity, value, 1.0), 0, 1)
            result.append(-TIME_STEP * change.reshape(64, 128).T)
        return result

    before_x, own_x, after_x = maps(True)
    before_y, own_y, after_y = maps(False)
    eye = np.eye(64)
    own_x[:64] += eye
    own_x[:64] -= TIME_STEP * (table[0, 0] - 6.0 * (0.5 - 0.5 - 1.0)) * eye
    low = -TIME_STEP * -6.0 * (0.5 + 0.5) * eye
    near_a = np.concatenate([low, -TIME_STEP * table[0, 1] * eye])
    near_b = np.concatenate([-TIME_STEP * table[0, 2] * eye, -TIME_STEP * table[0, 3] * eye])
    every = [own_x, own_y, near_a, near_b, before_x, after_x, before_y, after_y]
    return np.concatenate(every).astype(np.float32)


def tile_kernel(state_ref, tile_ref):
    at = 4 * (state_ref.shape[2] // 8)
    pick = lax.broadcasted_iota(jnp.int32, (8, 128), 1) == (
        lax.broadcasted_iota(jnp.int32, (8, 128), 0) + (at - 1)
    )
    pick = pick.astype(jnp.float32)

    def points(field):
        return lax.dot_general(
            pick, field, (((1,), (1,)), ((), ())),
            precision=lax.Precision.HIGHEST, preferred_element_type=jnp.float32,
        )

    value = points(state_ref[3] + state_ref[4])
    axial = points(state_ref[1])
    azimuthal = points(state_ref[2])
    rows = [
        jnp.concatenate([value[1:2], axial[1:2]], axis=1),
        jnp.concatenate([value[1:2], azimuthal[1:2]], axis=1),
        jnp.concatenate([value[0:1], value[2:3]], axis=1),
        jnp.concatenate([value[3:4], value[4:5]], axis=1),
        jnp.zeros((4, 128), jnp.float32),
    ]
    tile_ref[...] = jnp.concatenate(rows, axis=0)


def source_kernel(map_ref, own_ref, bx_ref, ax_ref, by_ref, ay_ref, index_ref, count_ref, source_ref):
    rows = [own_ref[0:1], own_ref[1:2], own_ref[2:3], own_ref[3:4],
            bx_ref[0:1], ax_ref[0:1], by_ref[1:2], ay_ref[1:2]]
    exact = dict(precision=lax.Precision.HIGHEST, preferred_element_type=jnp.float32)
    plane = jnp.dot(jnp.concatenate(rows, axis=1), map_ref[...], **exact)
    points = lax.broadcasted_iota(jnp.int32, (64, SLOTS), 0)
    hit = (index_ref[...] == points).astype(jnp.float32)
    source = jnp.dot(plane, hit, **exact)
    live = lax.broadcasted_iota(jnp.int32, (1, SLOTS), 1) < count_ref[0, 0]
    source_ref[...] = jnp.where(live, source, 0.0)


def slot_source(state, surf_index, surf_count):
    vmem = pl.BlockSpec(memory_space=pltpu.VMEM)
    tile = pl.pallas_call(
        tile_kernel,
        in_specs=[vmem],
        out_specs=vmem,
        out_shape=jax.ShapeDtypeStruct((8, 128), jnp.float32),
        name="tile",
    )(state.reshape(5, 64, state.shape[3]))

    def around(axes, size, wrap):
        up = [(i, (i + 1) % size) for i in range(size if wrap else size - 1)]
        down = [(j, i) for i, j in up]
        return lax.ppermute(tile, axes, up), lax.ppermute(tile, axes, down)

    before_x, after_x = around(AXIAL, lax.axis_size(AXIAL), False)
    before_y, after_y = around(AZIMUTHAL, lax.axis_size(AZIMUTHAL), True)
    return pl.pallas_call(
        source_kernel,
        in_specs=[vmem] * 7 + [pl.BlockSpec(memory_space=pltpu.SMEM)],
        out_specs=vmem,
        out_shape=jax.ShapeDtypeStruct((1, SLOTS), jnp.float32),
        name="source",
    )(
        jnp.asarray(line_operators()), tile, before_x, after_x, before_y, after_y,
        surf_index.reshape(1, SLOTS), surf_count,
    )


def half_kernel(core_ref, delay_ref, fraction_ref, delay_out, fraction_out):
    delay_out[...] = delay_ref[...]
    fraction_out[...] = fraction_ref[...]


def other_half(core, delay, fraction):
    width = delay.shape[1] // 8
    taken = pl.BlockSpec((SLOTS, width), lambda n, c: (0, 2 * n + 1 - c[0]))
    given = pl.BlockSpec((SLOTS, width), lambda n, c: (0, n))
    return pl.pallas_call(
        half_kernel,
        grid_spec=pltpu.PrefetchScalarGridSpec(
            num_scalar_prefetch=1, grid=(4,), in_specs=[taken] * 2, out_specs=[given] * 2
        ),
        out_shape=[
            jax.ShapeDtypeStruct((SLOTS, 4 * width), jnp.int32),
            jax.ShapeDtypeStruct((SLOTS, 4 * width), jnp.float32),
        ],
        name="other_half",
    )(core, delay, fraction)


def bins_kernel(core_ref, src_ref, src_b_ref, da_ref, fa_ref, db_ref, fb_ref, out_ref, d_t, f_t, hi_s, *, unroll=2):
    def flip(a_ref, b_ref, dst, cast):
        for n, (r, base) in enumerate(((a_ref, 0), (a_ref, 128), (b_ref, 0), (b_ref, 128))):
            dst[:, n * 128:(n + 1) * 128] = cast(r[base:base + 128, :]).T
        rest = jnp.concatenate([cast(a_ref[256:272, :]), cast(b_ref[256:272, :]), jnp.zeros((96, 128), jnp.float32)], axis=0)
        dst[:, 512:640] = rest.T
    flip(da_ref, db_ref, d_t, lambda v: v.astype(jnp.float32))
    flip(fa_ref, fb_ref, f_t, lambda v: v)
    src = jnp.concatenate(
        [src_ref[:, :256], src_b_ref[:, :256], src_ref[:, 256:], src_b_ref[:, 256:],
         jnp.zeros((1, 96), jnp.float32)], axis=1)
    row16 = lax.broadcasted_iota(jnp.int32, (16, LANES), 0)
    half = (row16 >= 8).astype(jnp.float32)
    count_lo = row16.astype(jnp.float32).astype(jnp.bfloat16)
    count_up = (row16 + 16).astype(jnp.float32).astype(jnp.bfloat16)
    one = jnp.ones((16, LANES), jnp.bfloat16)
    zero = jnp.zeros((16, LANES), jnp.bfloat16)
    lane = lax.broadcasted_iota(jnp.int32, (32, 128), 1) & 7
    lane8 = lax.broadcasted_iota(jnp.int32, (8, 128), 1) & 7
    diag8 = lane8 == lax.broadcasted_iota(jnp.int32, (8, 128), 0)

    def group(g, slot):
        rows = pl.ds(pl.multiple_of(g * 8, 8), 8)
        k = d_t[rows, :]
        f = f_t[rows, :]
        c = src * (25.6 / (512.0 + k))
        up = f * c
        low = c - up
        hi = jnp.floor((k + 0.5) * (1.0 / 15.0))
        lo = k - 15.0 * hi
        hi_s[slot] = hi
        twice = lambda v: jnp.concatenate([v, v], axis=0)
        lo2 = (twice(lo) - half).astype(jnp.bfloat16)
        hi2 = (twice(hi) - half).astype(jnp.bfloat16)
        def parts(v):
            top = v.astype(jnp.bfloat16)
            rest = (v - top.astype(jnp.float32))
            return twice(v).astype(jnp.bfloat16), twice(rest).astype(jnp.bfloat16)
        low_a, low_b = parts(low)
        up_a, up_b = parts(up)
        wa, wb = [], []
        for j in range(0, 16, 2):
            at = lo2 == jnp.bfloat16(j)
            before = lo2 == jnp.bfloat16(j - 1)
            wa.append(jnp.where(at, low_a, jnp.where(before, up_a, zero)))
            wb.append(jnp.where(at, low_b, jnp.where(before, up_b, zero)))
        w = jnp.concatenate(wa + wb, axis=0)
        h = []
        for o in range(8):
            row = jnp.broadcast_to(hi_s[slot, o:o + 1, :], (16, LANES)).astype(jnp.bfloat16)
            h.append(jnp.where(row == count_lo, one, zero))
            h.append(jnp.where(row == count_up, one, zero))
        h.append(jnp.where(hi2 == jnp.bfloat16(32), one, zero))
        h.append(jnp.where(hi2 == jnp.bfloat16(34), one, zero))
        h = jnp.concatenate(h, axis=0)
        r = lax.dot_general(h, w, (((1,), (1,)), ((), ())), preferred_element_type=jnp.float32)
        r = r[:, :128] + r[:, 128:]
        main = r[0:32]
        for o in range(1, 8):
            main = jnp.where(lane == o, r[32 * o:32 * o + 32], main)
        extra = [jnp.sum(jnp.where(diag8, r[256 + 8 * e:264 + 8 * e], 0.0), axis=0, keepdims=True) for e in range(4)]
        return jnp.concatenate([main] + extra, axis=0)

    def pair(p, _):
        two = [group(2 * p + t, t) for t in range(2)]
        out_ref[p] = jnp.concatenate(two, axis=0)
        return 0
    lax.fori_loop(0, BLOCK // 16, pair, 0, unroll=False)

def bins(place, src, src_b, delay, frac, delay_b, frac_b):
    mine = pl.BlockSpec((SLOTS, BLOCK), lambda n, c: (0, c[1] * 4 + c[0] * 2 + n))
    other = pl.BlockSpec((SLOTS, BLOCK), lambda n, c: (0, c[1] * 2 + n))
    row = pl.BlockSpec((1, SLOTS), lambda n, c: (0, 0))
    owners = 256 // 16
    return pl.pallas_call(
        bins_kernel,
        grid_spec=pltpu.PrefetchScalarGridSpec(
            num_scalar_prefetch=1,
            grid=(256 // BLOCK,),
            in_specs=[row, row, mine, mine, other, other],
            out_specs=pl.BlockSpec((BLOCK // 16, 2 * ROWS, 128), lambda n, c: (n, 0, 0)),
            scratch_shapes=[
                pltpu.VMEM((BLOCK, LANES), jnp.float32),
                pltpu.VMEM((BLOCK, LANES), jnp.float32),
                pltpu.VMEM((2, 8, LANES), jnp.float32),
            ],
        ),
        out_shape=jax.ShapeDtypeStruct((owners, 2 * ROWS, 128), jnp.float32),
        compiler_params=pltpu.CompilerParams(vmem_limit_bytes=32 * 1024 * 1024),
        cost_estimate=pl.CostEstimate(
            flops=32 * 2 * 288 * 256 * LANES, bytes_accessed=8 * 2 * SLOTS * 256, transcendentals=0
        ),
        name="bins",
    )(place, src, src_b, delay, frac, delay_b, frac_b)


def shifted(array, axis, step):
    return lax.ppermute(array, axis, [(i, (i + step) % 4) for i in range(4)])


def scattered(total, axis):
    here = lax.axis_index(axis)
    block = lambda d: lax.dynamic_index_in_dim(total, (here + d) % 4, 0, keepdims=False)
    got = [shifted(block(d), axis, d) for d in (2, 1, 3)]
    return block(0) + got[0] + got[1] + got[2]


def local(state, surf_index, surf_count, delay, fraction):
    core = lax.axis_index("core").reshape(1)
    swap = [(0, 1), (1, 0)]
    delay_b, fraction_b = other_half(core, delay, fraction)
    delay_b = lax.ppermute(delay_b, "core", swap)
    fraction_b = lax.ppermute(fraction_b, "core", swap)
    source = slot_source(state, surf_index, surf_count)
    source_b = lax.ppermute(source, "core", swap)
    here = lax.axis_index("x")
    got = []
    for d in (2, 1, 3, 0):
        place = jnp.stack([core[0], (here + d) % 4])
        sums = bins(place, source, source_b, delay, fraction, delay_b, fraction_b)
        got.append(shifted(sums, "x", d) if d else sums)
    total = (got[0] + got[1] + got[2] + got[3]).reshape(4, 4, 2 * ROWS, 128)
    total = scattered(scattered(total, "y"), "z")
    total = total.reshape(2, ROWS, 16, 8).transpose(0, 3, 1, 2).reshape(16, ROWS, 16)
    carry = jnp.pad(total[:, :34, 15:], ((0, 0), (1, 0), (0, 14)))
    return (total[:, :35, :RADIX] + carry).reshape(16, 35 * RADIX)[:, :SAMPLES]


def solution(mesh):
    fine = Mesh(mesh.devices.reshape(4, 2, 4, 4), ("x", "core", "y", "z"))
    ax, az = ("x", "core"), ("y", "z")
    placed = (
        P(None, ax, az, None),
        P(ax + az),
        P(ax, az),
        P(ax + az, None),
        P(ax + az, None),
    )
    return jax.shard_map(
        local, mesh=fine, in_specs=placed, out_specs=P(ax + az, None), check_vma=False
    )
```

```python
import jax
import jax.numpy as jnp
import numpy as np
from jax import lax
from jax.experimental import pallas as pl
from jax.experimental.pallas import tpu as pltpu
from jax.sharding import Mesh
from jax.sharding import PartitionSpec as P

SLOTS = 272
LANES = 640
RADIX = 15
ROWS = 36
UNROLL = 16
SAMPLES = 512
ORDER = (("x", "y", "z"), ("z", "x", "y"))
AXIAL = ("x", "core")
AZIMUTHAL = ("y", "z")
MEAN_FLOW = 0.5
TIME_STEP = 0.05


def lobatto_matrix():
    points = np.array([-1.0, -1.0 / np.sqrt(5.0), 1.0 / np.sqrt(5.0), 1.0])
    table = np.zeros((4, 4))
    for i in range(4):
        for j in range(4):
            if i == j:
                table[i, j] = sum((1.0 / (points[i] - points[m]) for m in range(4) if m != i))
            else:
                a = np.prod([points[i] - points[m] for m in range(4) if m != i])
                b = np.prod([points[j] - points[m] for m in range(4) if m != j])
                table[i, j] = a / (b * (points[i] - points[j]))
    return table


def line_operators():
    table = lobatto_matrix()

    def derivative(flux, value, speed):
        out = np.zeros((8,) + flux.shape[1:])
        for start in (1, 5):
            def common(low):
                mean = 0.5 * (flux[low] + flux[low + 1])
                return mean - 0.5 * speed * (value[low + 1] - value[low])
            for i in range(4):
                out[start - 1 + i] = sum(table[i, j] * flux[start + j] for j in range(4))
            out[start + 2] += 6.0 * (common(start + 3) - flux[start + 3])
            out[start - 1] -= 6.0 * (common(start - 1) - flux[start])
        return out

    def maps(along_axial):
        result = []
        for place in range(3):
            unit = np.zeros((24, 8, 128))
            for point in range(64):
                line, other = (point // 8, point % 8) if along_axial else (point % 8, point // 8)
                unit[place * 8 + line, other, point] = 1.0
            value = unit[7:17]
            speed_of = np.zeros((24, 8, 128))
            for point in range(64):
                line, other = (point // 8, point % 8) if along_axial else (point % 8, point // 8)
                speed_of[place * 8 + line, other, 64 + point] = 1.0
            velocity = speed_of[7:17]
            if along_axial:
                change = derivative(MEAN_FLOW * value + velocity, value, 1.5)
            else:
                change = np.swapaxes(derivative(velocity, value, 1.0), 0, 1)
            result.append(-TIME_STEP * change.reshape(64, 128).T)
        return result

    before_x, own_x, after_x = maps(True)
    before_y, own_y, after_y = maps(False)
    eye = np.eye(64)
    own_x[:64] += eye
    own_x[:64] -= TIME_STEP * (table[0, 0] - 6.0 * (0.5 - 0.5 - 1.0)) * eye
    low = -TIME_STEP * -6.0 * (0.5 + 0.5) * eye
    near_a = np.concatenate([low, -TIME_STEP * table[0, 1] * eye])
    near_b = np.concatenate([-TIME_STEP * table[0, 2] * eye, -TIME_STEP * table[0, 3] * eye])
    every = [own_x, own_y, near_a, near_b, before_x, after_x, before_y, after_y]
    return np.concatenate(every).astype(np.float32)


def tile_kernel(state_ref, tile_ref):
    at = 4 * (state_ref.shape[2] // 8)
    pick = lax.broadcasted_iota(jnp.int32, (8, 128), 1) == (
        lax.broadcasted_iota(jnp.int32, (8, 128), 0) + (at - 1)
    )
    pick = pick.astype(jnp.float32)

    def points(field):
        return lax.dot_general(
            pick, field, (((1,), (1,)), ((), ())),
            precision=lax.Precision.HIGHEST, preferred_element_type=jnp.float32,
        )

    value = points(state_ref[3] + state_ref[4])
    axial = points(state_ref[1])
    azimuthal = points(state_ref[2])
    rows = [
        jnp.concatenate([value[1:2], axial[1:2]], axis=1),
        jnp.concatenate([value[1:2], azimuthal[1:2]], axis=1),
        jnp.concatenate([value[0:1], value[2:3]], axis=1),
        jnp.concatenate([value[3:4], value[4:5]], axis=1),
        jnp.zeros((4, 128), jnp.float32),
    ]
    tile_ref[...] = jnp.concatenate(rows, axis=0)


def source_kernel(map_ref, own_ref, bx_ref, ax_ref, by_ref, ay_ref, index_ref, count_ref, source_ref):
    rows = [own_ref[0:1], own_ref[1:2], own_ref[2:3], own_ref[3:4],
            bx_ref[0:1], ax_ref[0:1], by_ref[1:2], ay_ref[1:2]]
    exact = dict(precision=lax.Precision.HIGHEST, preferred_element_type=jnp.float32)
    plane = jnp.dot(jnp.concatenate(rows, axis=1), map_ref[...], **exact)
    points = lax.broadcasted_iota(jnp.int32, (64, SLOTS), 0)
    hit = (index_ref[...] == points).astype(jnp.float32)
    source = jnp.dot(plane, hit, **exact)
    live = lax.broadcasted_iota(jnp.int32, (1, SLOTS), 1) < count_ref[0, 0]
    source_ref[...] = jnp.where(live, source, 0.0)


def slot_source(state, surf_index, surf_count):
    vmem = pl.BlockSpec(memory_space=pltpu.VMEM)
    tile = pl.pallas_call(
        tile_kernel,
        in_specs=[vmem],
        out_specs=vmem,
        out_shape=jax.ShapeDtypeStruct((8, 128), jnp.float32),
        name="tile",
    )(state.reshape(5, 64, state.shape[3]))

    def around(axes, size, wrap):
        up = [(i, (i + 1) % size) for i in range(size if wrap else size - 1)]
        down = [(j, i) for i, j in up]
        return lax.ppermute(tile, axes, up), lax.ppermute(tile, axes, down)

    before_x, after_x = around(AXIAL, lax.axis_size(AXIAL), False)
    before_y, after_y = around(AZIMUTHAL, lax.axis_size(AZIMUTHAL), True)
    return pl.pallas_call(
        source_kernel,
        in_specs=[vmem] * 7 + [pl.BlockSpec(memory_space=pltpu.SMEM)],
        out_specs=vmem,
        out_shape=jax.ShapeDtypeStruct((1, SLOTS), jnp.float32),
        name="source",
    )(
        jnp.asarray(line_operators()), tile, before_x, after_x, before_y, after_y,
        surf_index.reshape(1, SLOTS), surf_count,
    )


def turn_kernel(core_ref, own_delay, own_fraction, other_delay, other_fraction, own_ref, other_ref):
    for delay, fraction, out in (
        (own_delay, own_fraction, own_ref),
        (other_delay, other_fraction, other_ref),
    ):
        for at in (0, 128):
            rows = slice(at, at + 128)
            for base in (0, 128):
                out[rows, base : base + 128] = delay[base : base + 128, rows].astype(jnp.float32).T
                out[rows, 256 + base : 384 + base] = fraction[base : base + 128, rows].T
            rest = [
                delay[256:272, rows].astype(jnp.float32),
                fraction[256:272, rows],
                jnp.zeros((96, 128), jnp.float32),
            ]
            out[rows, 512:640] = jnp.concatenate(rest, axis=0).T


def turned(core, delay, fraction):
    mine = pl.BlockSpec((SLOTS, 256), lambda n, c: (0, 2 * n + c[0]))
    other = pl.BlockSpec((SLOTS, 256), lambda n, c: (0, 2 * n + 1 - c[0]))
    shape = jax.ShapeDtypeStruct((1024, LANES), jnp.float32)
    return pl.pallas_call(
        turn_kernel,
        grid_spec=pltpu.PrefetchScalarGridSpec(
            num_scalar_prefetch=1,
            grid=(4,),
            in_specs=[mine, mine, other, other],
            out_specs=[pl.BlockSpec((256, LANES), lambda n, c: (n, 0))] * 2,
        ),
        out_shape=[shape, shape],
        compiler_params=pltpu.CompilerParams(vmem_limit_bytes=32 * 1024 * 1024),
        name="turned",
    )(core, delay, fraction, delay, fraction)


def bins_kernel(part_ref, src_ref, src_b_ref, own_ref, sib_ref, out_ref, hi_s):
    src = jnp.concatenate(
        [src_ref[:, :256], src_b_ref[:, :256], src_ref[:, 256:], src_b_ref[:, 256:],
         jnp.zeros((1, 96), jnp.float32)], axis=1)
    first16 = lax.broadcasted_iota(jnp.int32, (8, 128), 1) < 16
    row16 = lax.broadcasted_iota(jnp.int32, (16, LANES), 0)
    half = (row16 >= 8).astype(jnp.float32)
    count_lo = row16.astype(jnp.float32).astype(jnp.bfloat16)
    count_up = (row16 + 16).astype(jnp.float32).astype(jnp.bfloat16)
    one = jnp.ones((16, LANES), jnp.bfloat16)
    zero = jnp.zeros((16, LANES), jnp.bfloat16)
    lane = lax.broadcasted_iota(jnp.int32, (32, 128), 1) & 7
    lane8 = lax.broadcasted_iota(jnp.int32, (8, 128), 1) & 7
    diag8 = lane8 == lax.broadcasted_iota(jnp.int32, (8, 128), 0)

    def group(g, slot):
        row = part_ref[0] + (g // 8) * part_ref[1] + (g // 2 % 4) * part_ref[2] + (g % 2) * 8
        rows = pl.ds(pl.multiple_of(row, 8), 8)
        last, last_b = own_ref[rows, 512:], sib_ref[rows, 512:]
        last_k = jnp.where(first16, last, pltpu.roll(last_b, 16, 1))
        last_f = jnp.where(first16, pltpu.roll(last, 112, 1), last_b)
        k = jnp.concatenate([own_ref[rows, :256], sib_ref[rows, :256], last_k], axis=1)
        f = jnp.concatenate([own_ref[rows, 256:512], sib_ref[rows, 256:512], last_f], axis=1)
        c = src * (25.6 / (512.0 + k))
        up = f * c
        low = c - up
        hi = jnp.floor((k + 0.5) * (1.0 / 15.0))
        lo = k - 15.0 * hi
        hi_s[slot] = hi
        twice = lambda v: jnp.concatenate([v, v], axis=0)
        lo2 = (twice(lo) - half).astype(jnp.bfloat16)
        hi2 = (twice(hi) - half).astype(jnp.bfloat16)
        def parts(v):
            top = v.astype(jnp.bfloat16)
            rest = (v - top.astype(jnp.float32))
            return twice(v).astype(jnp.bfloat16), twice(rest).astype(jnp.bfloat16)
        low_a, low_b = parts(low)
        up_a, up_b = parts(up)
        wa, wb = [], []
        for j in range(0, 16, 2):
            at = lo2 == jnp.bfloat16(j)
            before = lo2 == jnp.bfloat16(j - 1)
            wa.append(jnp.where(at, low_a, jnp.where(before, up_a, zero)))
            wb.append(jnp.where(at, low_b, jnp.where(before, up_b, zero)))
        w = jnp.concatenate(wa + wb, axis=0)
        h = []
        for o in range(8):
            row = jnp.broadcast_to(hi_s[slot, o:o + 1, :], (16, LANES)).astype(jnp.bfloat16)
            h.append(jnp.where(row == count_lo, one, zero))
            h.append(jnp.where(row == count_up, one, zero))
        h.append(jnp.where(hi2 == jnp.bfloat16(32), one, zero))
        h.append(jnp.where(hi2 == jnp.bfloat16(34), one, zero))
        h = jnp.concatenate(h, axis=0)
        r = lax.dot_general(h, w, (((1,), (1,)), ((), ())), preferred_element_type=jnp.float32)
        r = r[:, :128] + r[:, 128:]
        main = r[0:32]
        for o in range(1, 8):
            main = jnp.where(lane == o, r[32 * o:32 * o + 32], main)
        extra = [jnp.sum(jnp.where(diag8, r[256 + 8 * e:264 + 8 * e], 0.0), axis=0, keepdims=True) for e in range(4)]
        return jnp.concatenate([main] + extra, axis=0)

    def several(p, _):
        for t in range(0, UNROLL, 2):
            g = UNROLL * p + t
            out_ref[g // 2] = jnp.concatenate([group(g, t), group(g + 1, t + 1)], axis=0)
        return 0

    lax.fori_loop(0, 32 // UNROLL, several, 0)


def bins(part, src, src_b, own, sibling):
    vmem = pl.BlockSpec(memory_space=pltpu.VMEM)
    return pl.pallas_call(
        bins_kernel,
        in_specs=[pl.BlockSpec(memory_space=pltpu.SMEM)] + [vmem] * 4,
        out_specs=vmem,
        scratch_shapes=[pltpu.VMEM((UNROLL, 8, LANES), jnp.float32)],
        out_shape=jax.ShapeDtypeStruct((16, 2 * ROWS, 128), jnp.float32),
        compiler_params=pltpu.CompilerParams(vmem_limit_bytes=32 * 1024 * 1024),
        cost_estimate=pl.CostEstimate(
            flops=32 * 2 * 288 * 256 * LANES, bytes_accessed=8 * 256 * LANES, transcendentals=0
        ),
        name="bins",
    )(part, src, src_b, own, sibling)


def shifted(array, phase, step):
    moves = []
    for i in range(128):
        at = {"x": i // 32, "core": i // 16 % 2, "y": i // 4 % 4, "z": i % 4}
        axis = ORDER[at["core"]][phase]
        at[axis] = (at[axis] + step) % 4
        moves.append((i, at["x"] * 32 + at["core"] * 16 + at["y"] * 4 + at["z"]))
    return lax.ppermute(array, AXIAL + AZIMUTHAL, moves)


def summed(source, source_b, own, sibling):
    core = lax.axis_index("core")
    pick = lambda of: jnp.where(core == 0, of(ORDER[0]), of(ORDER[1]))
    here = [pick(lambda order: lax.axis_index(order[phase])) for phase in range(3)]
    rows = {"x": 256, "y": 64, "z": 16}
    steps = [pick(lambda order: rows[order[phase]]) for phase in range(3)]
    got = []
    for d in (2, 1, 3, 0):
        part = jnp.stack([(here[0] + d) % 4 * steps[0], steps[1], steps[2]]).astype(jnp.int32)
        sums = bins(part, source, source_b, own, sibling)
        got.append(shifted(sums, 0, d) if d else sums)
    total = (got[0] + got[1] + got[2] + got[3]).reshape(4, 4, 2 * ROWS, 128)
    for phase in (1, 2):
        block = lambda d: lax.dynamic_index_in_dim(total, (here[phase] + d) % 4, 0, keepdims=False)
        got = [shifted(block(d), phase, d) for d in (2, 1, 3)]
        total = block(0) + got[0] + got[1] + got[2]
    return total


def local(state, surf_index, surf_count, delay, fraction):
    core = lax.axis_index("core").reshape(1)
    swap = [(0, 1), (1, 0)]
    own, other = turned(core, delay, fraction)
    sibling = lax.ppermute(other, "core", swap)
    source = slot_source(state, surf_index, surf_count)
    source_b = lax.ppermute(source, "core", swap)
    total = summed(source, source_b, own, sibling)
    total = total.reshape(2, ROWS, 16, 8).transpose(0, 3, 1, 2).reshape(16, ROWS, 16)
    carry = jnp.pad(total[:, :34, 15:], ((0, 0), (1, 0), (0, 14)))
    return (total[:, :35, :RADIX] + carry).reshape(16, 35 * RADIX)[:, :SAMPLES]


def solution(mesh):
    fine = Mesh(mesh.devices.reshape(4, 2, 4, 4), ("x", "core", "y", "z"))
    ax, az = ("x", "core"), ("y", "z")
    placed = (
        P(None, ax, az, None),
        P(ax + az),
        P(ax, az),
        P(ax + az, None),
        P(ax + az, None),
    )
    return jax.shard_map(
        local, mesh=fine, in_specs=placed, out_specs=P(ax + az, None), check_vma=False
    )
```

```python
import jax
import jax.numpy as jnp
import numpy as np
from jax import lax
from jax.experimental import pallas as pl
from jax.experimental.pallas import tpu as pltpu
from jax.sharding import Mesh
from jax.sharding import PartitionSpec as P

SLOTS = 272
LANES = 640
RADIX = 15
ROWS = 36
UNROLL = 16
SAMPLES = 512
ORDER = (("x", "y", "z"), ("z", "x", "y"))
AXIAL = ("x", "core")
AZIMUTHAL = ("y", "z")
MEAN_FLOW = 0.5
TIME_STEP = 0.05


def lobatto_matrix():
    points = np.array([-1.0, -1.0 / np.sqrt(5.0), 1.0 / np.sqrt(5.0), 1.0])
    table = np.zeros((4, 4))
    for i in range(4):
        for j in range(4):
            if i == j:
                table[i, j] = sum((1.0 / (points[i] - points[m]) for m in range(4) if m != i))
            else:
                a = np.prod([points[i] - points[m] for m in range(4) if m != i])
                b = np.prod([points[j] - points[m] for m in range(4) if m != j])
                table[i, j] = a / (b * (points[i] - points[j]))
    return table


def in_vmem(*arrays):
    return [pltpu.with_memory_space_constraint(array, pltpu.VMEM) for array in arrays]


def first_kernel(core_ref, state_ref, own_delay, own_fraction, other_delay, other_fraction, own_ref, other_ref, tile_ref):
    for delay, fraction, out in (
        (own_delay, own_fraction, own_ref),
        (other_delay, other_fraction, other_ref),
    ):
        for at in (0, 128):
            rows = slice(at, at + 128)
            for base in (0, 128):
                out[rows, base : base + 128] = delay[base : base + 128, rows].astype(jnp.float32).T
                out[rows, 256 + base : 384 + base] = fraction[base : base + 128, rows].T
            rest = [
                delay[256:272, rows].astype(jnp.float32),
                fraction[256:272, rows],
                jnp.zeros((96, 128), jnp.float32),
            ]
            out[rows, 512:640] = jnp.concatenate(rest, axis=0).T

    @pl.when(pl.program_id(0) == 0)
    def _():
        at = 4 * (state_ref.shape[2] // 8)
        value = state_ref[3] + state_ref[4]
        axial = jnp.concatenate([value, state_ref[1]], axis=0).T[at - 8 : at + 8]
        azimuthal = jnp.concatenate([value, state_ref[2]], axis=0).T[at : at + 8]
        first = lax.broadcasted_iota(jnp.int32, (1, 128), 1) < 64
        after = pltpu.roll(axial, 64, 1)
        rows = [
            axial[8:9],
            azimuthal[0:1],
            jnp.where(first, axial[7:8], after[9:10]),
            jnp.where(first, axial[10:11], after[11:12]),
            jnp.zeros((4, 128), jnp.float32),
        ]
        tile_ref[...] = jnp.concatenate(rows, axis=0)


def first(core, state, delay, fraction):
    mine = pl.BlockSpec((SLOTS, 256), lambda n, c: (0, 2 * n + c[0]))
    other = pl.BlockSpec((SLOTS, 256), lambda n, c: (0, 2 * n + 1 - c[0]))
    state = state.reshape(5, 64, state.shape[3])
    delay, fraction, state = (
        pltpu.with_memory_space_constraint(array, pltpu.HBM) for array in (delay, fraction, state)
    )
    return pl.pallas_call(
        first_kernel,
        grid_spec=pltpu.PrefetchScalarGridSpec(
            num_scalar_prefetch=1,
            grid=(4,),
            in_specs=[pl.BlockSpec(state.shape, lambda n, c: (0, 0, 0)), mine, mine, other, other],
            out_specs=[pl.BlockSpec((256, LANES), lambda n, c: (n, 0))] * 2
            + [pl.BlockSpec((8, 128), lambda n, c: (0, 0))],
        ),
        out_shape=[
            pltpu.VMEM((1024, LANES), jnp.float32),
            pltpu.VMEM((1024, LANES), jnp.float32),
            pltpu.VMEM((8, 128), jnp.float32),
        ],
        compiler_params=pltpu.CompilerParams(vmem_limit_bytes=32 * 1024 * 1024),
        name="first",
    )(core, state, delay, fraction, delay, fraction)


def by_node(node, values):
    out = jnp.full(node.shape, values[0], jnp.float32)
    for n in (1, 2, 3):
        out = jnp.where(node == n, jnp.float32(values[n]), out)
    return out


def source_kernel(place_ref, own_ref, core_ref, chip_ref, even_ref, odd_ref, index_ref, count_ref, source_ref):
    table = lobatto_matrix()
    point = lax.broadcasted_iota(jnp.int32, (1, 128), 1)
    axial, azimuthal = point // 8, point % 8
    second = place_ref[0] == 1
    odd = place_ref[1] == 1
    no_before, no_after = place_ref[2] == 0, place_ref[2] == 7
    core, chip = core_ref[...], chip_ref[...]
    before_x = jnp.where(no_before, 0.0, jnp.where(second, core, chip))[0:1]
    after_x = jnp.where(no_after, 0.0, jnp.where(second, chip, core))[0:1]
    even, odd_tile = even_ref[...], odd_ref[...]
    before_y = jnp.where(odd, even, odd_tile)[1:2]
    after_y = jnp.where(odd, odd_tile, even)[1:2]

    def to_lane(array, shift):
        return pltpu.roll(array, shift % 128, 1)

    def split(row, mean):
        value, velocity = row, to_lane(row, -64)
        return (MEAN_FLOW * value if mean else 0.0) + velocity, value

    def derivative(own, before, after, width, coordinate, speed, mean):
        node = coordinate % 4
        flux, value = split(own, mean)
        out = 0.0
        for shift in range(-3, 4):
            weights = [table[n, n + shift] if 0 <= n + shift < 4 else 0.0 for n in range(4)]
            moved = flux if shift == 0 else to_lane(flux, -shift * width)
            out = out + by_node(node, weights) * moved
        sides = []
        for outside, end, step, back in ((after, 7, -width, 7 * width), (before, 0, width, -7 * width)):
            there_flux, there_value = split(outside, mean)
            at_end = coordinate == end
            sides.append((
                jnp.where(at_end, to_lane(there_flux, back), to_lane(flux, step)),
                jnp.where(at_end, to_lane(there_value, back), to_lane(value, step)),
            ))
        (up_flux, up_value), (low_flux, low_value) = sides
        up = 0.5 * (flux + up_flux) - 0.5 * speed * (up_value - value)
        low = 0.5 * (low_flux + flux) - 0.5 * speed * (value - low_value)
        out = out + jnp.where(node == 3, 6.0 * (up - flux), 0.0)
        return out - jnp.where(node == 0, 6.0 * (low - flux), 0.0)

    own = own_ref[0:4]
    change = derivative(own[0:1], before_x, after_x, 8, axial, 1.5, True)
    change = change + derivative(own[1:2], before_y, after_y, 1, azimuthal, 1.0, False)
    value, lower = own[0:1], own[2:3]
    radial = (
        np.float32(table[0, 0]) * value
        + np.float32(table[0, 1]) * to_lane(own[2:3], -64)
        + np.float32(table[0, 2]) * own[3:4]
        + np.float32(table[0, 3]) * to_lane(own[3:4], -64)
    )
    common = 0.5 * (lower + value) - 0.5 * (value - lower)
    change = change + (radial - 6.0 * (common - value))
    plane = jnp.where(point < 64, value - TIME_STEP * change, 0.0)
    terms = []
    for _ in range(3):
        term = plane.astype(jnp.bfloat16).astype(jnp.float32)
        terms.append(term)
        plane = plane - term
    rows = jnp.concatenate(terms + [jnp.zeros((5, 128), jnp.float32)], axis=0).astype(jnp.bfloat16)
    points = lax.broadcasted_iota(jnp.int32, (128, SLOTS), 0)
    index = index_ref[...].reshape(1, SLOTS)
    hit = jnp.where(index == points, 1.0, 0.0).astype(jnp.bfloat16)
    source = jnp.dot(rows, hit, preferred_element_type=jnp.float32)
    source = source[0:1] + source[1:2] + source[2:3]
    live = lax.broadcasted_iota(jnp.int32, (1, SLOTS), 1) < count_ref[0, 0]
    source_ref[...] = jnp.where(live, source, 0.0)


def neighbour(kind):
    moves = []
    for i in range(128):
        axial, azimuthal = i // 16, i % 16
        if kind == "core":
            axial ^= 1
        elif kind == "chip":
            axial = (axial + 1 if axial % 2 else axial - 1) % 8
        elif kind == "even":
            azimuthal ^= 1
        else:
            azimuthal = (azimuthal + 1 if azimuthal % 2 else azimuthal - 1) % 16
        moves.append((i, axial * 16 + azimuthal))
    return moves


def slot_source(tile, surf_index, surf_count):
    tiles = [
        lax.ppermute(tile, AXIAL + AZIMUTHAL, neighbour(kind)) for kind in ("core", "chip", "even", "odd")
    ]
    axial = lax.axis_index(AXIAL)
    place = jnp.stack([axial % 2, lax.axis_index(AZIMUTHAL) % 2, axial]).astype(jnp.int32)
    vmem = pl.BlockSpec(memory_space=pltpu.VMEM)
    smem = pl.BlockSpec(memory_space=pltpu.SMEM)
    return pl.pallas_call(
        source_kernel,
        in_specs=[smem] + [vmem] * 6 + [smem],
        out_specs=vmem,
        out_shape=pltpu.VMEM((1, SLOTS), jnp.float32),
        name="source",
    )(place, *in_vmem(tile, *tiles, surf_index), surf_count)


def bins_kernel(part_ref, src_ref, src_b_ref, own_ref, sib_ref, out_ref, hi_s):
    src = jnp.concatenate(
        [src_ref[:, :256], src_b_ref[:, :256], src_ref[:, 256:], src_b_ref[:, 256:],
         jnp.zeros((1, 96), jnp.float32)], axis=1)
    first16 = lax.broadcasted_iota(jnp.int32, (8, 128), 1) < 16
    row16 = lax.broadcasted_iota(jnp.int32, (16, LANES), 0)
    half = (row16 >= 8).astype(jnp.float32)
    count_lo = row16.astype(jnp.float32).astype(jnp.bfloat16)
    count_up = (row16 + 16).astype(jnp.float32).astype(jnp.bfloat16)
    one = jnp.ones((16, LANES), jnp.bfloat16)
    zero = jnp.zeros((16, LANES), jnp.bfloat16)
    lane = lax.broadcasted_iota(jnp.int32, (32, 128), 1) & 7
    lane8 = lax.broadcasted_iota(jnp.int32, (8, 128), 1) & 7
    diag8 = lane8 == lax.broadcasted_iota(jnp.int32, (8, 128), 0)

    def group(g, slot):
        row = part_ref[0] + (g // 8) * part_ref[1] + (g // 2 % 4) * part_ref[2] + (g % 2) * 8
        rows = pl.ds(pl.multiple_of(row, 8), 8)
        last, last_b = own_ref[rows, 512:], sib_ref[rows, 512:]
        last_k = jnp.where(first16, last, pltpu.roll(last_b, 16, 1))
        last_f = jnp.where(first16, pltpu.roll(last, 112, 1), last_b)
        k = jnp.concatenate([own_ref[rows, :256], sib_ref[rows, :256], last_k], axis=1)
        f = jnp.concatenate([own_ref[rows, 256:512], sib_ref[rows, 256:512], last_f], axis=1)
        c = src * (25.6 / (512.0 + k))
        up = f * c
        low = c - up
        hi = jnp.floor((k + 0.5) * (1.0 / 15.0))
        lo = k - 15.0 * hi
        hi_s[slot] = hi
        twice = lambda v: jnp.concatenate([v, v], axis=0)
        lo2 = (twice(lo) - half).astype(jnp.bfloat16)
        hi2 = (twice(hi) - half).astype(jnp.bfloat16)
        def parts(v):
            top = v.astype(jnp.bfloat16)
            rest = (v - top.astype(jnp.float32))
            return twice(v).astype(jnp.bfloat16), twice(rest).astype(jnp.bfloat16)
        low_a, low_b = parts(low)
        up_a, up_b = parts(up)
        wa, wb = [], []
        for j in range(0, 16, 2):
            at = lo2 == jnp.bfloat16(j)
            before = lo2 == jnp.bfloat16(j - 1)
            wa.append(jnp.where(at, low_a, jnp.where(before, up_a, zero)))
            wb.append(jnp.where(at, low_b, jnp.where(before, up_b, zero)))
        w = jnp.concatenate(wa + wb, axis=0)
        h = []
        for o in range(8):
            row = jnp.broadcast_to(hi_s[slot, o:o + 1, :], (16, LANES)).astype(jnp.bfloat16)
            h.append(jnp.where(row == count_lo, one, zero))
            h.append(jnp.where(row == count_up, one, zero))
        h.append(jnp.where(hi2 == jnp.bfloat16(32), one, zero))
        h.append(jnp.where(hi2 == jnp.bfloat16(34), one, zero))
        h = jnp.concatenate(h, axis=0)
        r = lax.dot_general(h, w, (((1,), (1,)), ((), ())), preferred_element_type=jnp.float32)
        r = r[:, :128] + r[:, 128:]
        main = r[0:32]
        for o in range(1, 8):
            main = jnp.where(lane == o, r[32 * o:32 * o + 32], main)
        extra = [jnp.sum(jnp.where(diag8, r[256 + 8 * e:264 + 8 * e], 0.0), axis=0, keepdims=True) for e in range(4)]
        return jnp.concatenate([main] + extra, axis=0)

    def several(p, _):
        for t in range(0, UNROLL, 2):
            g = UNROLL * p + t
            out_ref[g // 2] = jnp.concatenate([group(g, t), group(g + 1, t + 1)], axis=0)
        return 0

    lax.fori_loop(0, 32 // UNROLL, several, 0)


def bins(part, src, src_b, own, sibling):
    vmem = pl.BlockSpec(memory_space=pltpu.VMEM)
    return pl.pallas_call(
        bins_kernel,
        in_specs=[pl.BlockSpec(memory_space=pltpu.SMEM)] + [vmem] * 4,
        out_specs=vmem,
        scratch_shapes=[pltpu.VMEM((UNROLL, 8, LANES), jnp.float32)],
        out_shape=pltpu.VMEM((16, 2 * ROWS, 128), jnp.float32),
        compiler_params=pltpu.CompilerParams(vmem_limit_bytes=32 * 1024 * 1024),
        cost_estimate=pl.CostEstimate(
            flops=32 * 2 * 288 * 256 * LANES, bytes_accessed=8 * 256 * LANES, transcendentals=0
        ),
        name="bins",
    )(part, *in_vmem(src, src_b, own, sibling))


def shifted(array, phase, step):
    moves = []
    for i in range(128):
        at = {"x": i // 32, "core": i // 16 % 2, "y": i // 4 % 4, "z": i % 4}
        axis = ORDER[at["core"]][phase]
        at[axis] = (at[axis] + step) % 4
        moves.append((i, at["x"] * 32 + at["core"] * 16 + at["y"] * 4 + at["z"]))
    return lax.ppermute(array, AXIAL + AZIMUTHAL, moves)


def summed(source, source_b, own, sibling):
    core = lax.axis_index("core")
    pick = lambda of: jnp.where(core == 0, of(ORDER[0]), of(ORDER[1]))
    here = [pick(lambda order: lax.axis_index(order[phase])) for phase in range(3)]
    rows = {"x": 256, "y": 64, "z": 16}
    steps = [pick(lambda order: rows[order[phase]]) for phase in range(3)]
    got = []
    for d in (2, 1, 3, 0):
        part = jnp.stack([(here[0] + d) % 4 * steps[0], steps[1], steps[2]]).astype(jnp.int32)
        sums = bins(part, source, source_b, own, sibling)
        got.append(shifted(sums, 0, d) if d else sums)
    total = (got[0] + got[1] + got[2] + got[3]).reshape(4, 4, 2 * ROWS, 128)
    for phase in (1, 2):
        block = lambda d: lax.dynamic_index_in_dim(total, (here[phase] + d) % 4, 0, keepdims=False)
        got = [shifted(block(d), phase, d) for d in (2, 1, 3)]
        total = block(0) + got[0] + got[1] + got[2]
    return total


def local(state, surf_index, surf_count, delay, fraction):
    core = lax.axis_index("core").reshape(1)
    swap = [(0, 1), (1, 0)]
    own, other, tile = first(core, state, delay, fraction)
    sibling = lax.ppermute(other, "core", swap)
    source = slot_source(tile, surf_index, surf_count)
    source_b = lax.ppermute(source, "core", swap)
    total = summed(source, source_b, own, sibling)
    total = total.reshape(2, ROWS, 16, 8).transpose(0, 3, 1, 2).reshape(16, ROWS, 16)
    carry = jnp.pad(total[:, :34, 15:], ((0, 0), (1, 0), (0, 14)))
    return (total[:, :35, :RADIX] + carry).reshape(16, 35 * RADIX)[:, :SAMPLES]


def solution(mesh):
    fine = Mesh(mesh.devices.reshape(4, 2, 4, 4), ("x", "core", "y", "z"))
    ax, az = ("x", "core"), ("y", "z")
    placed = (
        P(None, ax, az, None),
        P(ax + az),
        P(ax, az),
        P(ax + az, None),
        P(ax + az, None),
    )
    return jax.shard_map(
        local, mesh=fine, in_specs=placed, out_specs=P(ax + az, None), check_vma=False
    )
```

```python
import functools

import jax
import jax.numpy as jnp
import numpy as np
from jax import lax
from jax.experimental import pallas as pl
from jax.experimental.pallas import tpu as pltpu
from jax.sharding import Mesh
from jax.sharding import PartitionSpec as P

SLOTS = 272
LANES = 640
RADIX = 15
ROWS = 36
STEPS = (2, 1, 3, 0)
UNROLL = 16
SAMPLES = 512
ORDER = (("x", "y", "z"), ("y", "x", "z"))
AXIAL = ("x", "core")
AZIMUTHAL = ("y", "z")
MEAN_FLOW = 0.5
TIME_STEP = 0.05


def lobatto_matrix():
    points = np.array([-1.0, -1.0 / np.sqrt(5.0), 1.0 / np.sqrt(5.0), 1.0])
    table = np.zeros((4, 4))
    for i in range(4):
        for j in range(4):
            if i == j:
                table[i, j] = sum((1.0 / (points[i] - points[m]) for m in range(4) if m != i))
            else:
                a = np.prod([points[i] - points[m] for m in range(4) if m != i])
                b = np.prod([points[j] - points[m] for m in range(4) if m != j])
                table[i, j] = a / (b * (points[i] - points[j]))
    return table


def in_vmem(*arrays):
    return [pltpu.with_memory_space_constraint(array, pltpu.VMEM) for array in arrays]


def first_kernel(core_ref, state_ref, own_delay, own_fraction, other_delay, other_fraction, own_ref, other_ref, tile_ref):
    for delay, fraction, out in (
        (own_delay, own_fraction, own_ref),
        (other_delay, other_fraction, other_ref),
    ):
        for at in (0, 128):
            rows = slice(at, at + 128)
            for base in (0, 128):
                out[rows, base : base + 128] = delay[base : base + 128, rows].astype(jnp.float32).T
                out[rows, 256 + base : 384 + base] = fraction[base : base + 128, rows].T
            rest = [
                delay[256:272, rows].astype(jnp.float32),
                fraction[256:272, rows],
                jnp.zeros((96, 128), jnp.float32),
            ]
            out[rows, 512:640] = jnp.concatenate(rest, axis=0).T

    @pl.when(pl.program_id(0) == 0)
    def _():
        at = 4 * (state_ref.shape[2] // 8)
        value = state_ref[3] + state_ref[4]
        axial = jnp.concatenate([value, state_ref[1]], axis=0).T[at - 8 : at + 8]
        azimuthal = jnp.concatenate([value, state_ref[2]], axis=0).T[at : at + 8]
        first = lax.broadcasted_iota(jnp.int32, (1, 128), 1) < 64
        after = pltpu.roll(axial, 64, 1)
        rows = [
            axial[8:9],
            azimuthal[0:1],
            jnp.where(first, axial[7:8], after[9:10]),
            jnp.where(first, axial[10:11], after[11:12]),
            jnp.zeros((4, 128), jnp.float32),
        ]
        tile_ref[...] = jnp.concatenate(rows, axis=0)


def first(core, state, delay, fraction):
    mine = pl.BlockSpec((SLOTS, 256), lambda n, c: (0, 2 * n + c[0]))
    other = pl.BlockSpec((SLOTS, 256), lambda n, c: (0, 2 * n + 1 - c[0]))
    state = state.reshape(5, 64, state.shape[3])
    delay, fraction, state = (
        pltpu.with_memory_space_constraint(array, pltpu.HBM) for array in (delay, fraction, state)
    )
    return pl.pallas_call(
        first_kernel,
        grid_spec=pltpu.PrefetchScalarGridSpec(
            num_scalar_prefetch=1,
            grid=(4,),
            in_specs=[pl.BlockSpec(state.shape, lambda n, c: (0, 0, 0)), mine, mine, other, other],
            out_specs=[
                pl.BlockSpec((256, LANES), lambda n, c: (n, 0)),
                pl.BlockSpec((256, LANES), lambda n, c: (n, 0)),
                pl.BlockSpec((8, 128), lambda n, c: (0, 0)),
            ],
        ),
        out_shape=[
            jax.ShapeDtypeStruct((1024, LANES), jnp.float32),
            jax.ShapeDtypeStruct((1024, LANES), jnp.float32),
            pltpu.VMEM((8, 128), jnp.float32),
        ],
        compiler_params=pltpu.CompilerParams(vmem_limit_bytes=16 * 1024 * 1024),
        name="first",
    )(core, state, delay, fraction, delay, fraction)


def by_node(node, values):
    out = jnp.full(node.shape, values[0], jnp.float32)
    for n in (1, 2, 3):
        out = jnp.where(node == n, jnp.float32(values[n]), out)
    return out


def source_kernel(own_ref, core_ref, chip_ref, even_ref, odd_ref, index_ref, count_ref, source_ref):
    table = lobatto_matrix()
    point = lax.broadcasted_iota(jnp.int32, (1, 128), 1)
    axial, azimuthal = point // 8, point % 8
    x, core = lax.axis_index("x"), lax.axis_index("core")
    second = core == 1
    odd = lax.rem(lax.axis_index("z"), 2) == 1
    no_before, no_after = x * 2 + core == 0, x * 2 + core == 7
    core_tile, chip = core_ref[...], chip_ref[...]
    before_x = jnp.where(no_before, 0.0, jnp.where(second, core_tile, chip))[0:1]
    after_x = jnp.where(no_after, 0.0, jnp.where(second, chip, core_tile))[0:1]
    even, odd_tile = even_ref[...], odd_ref[...]
    before_y = jnp.where(odd, even, odd_tile)[1:2]
    after_y = jnp.where(odd, odd_tile, even)[1:2]

    def to_lane(array, shift):
        return pltpu.roll(array, shift % 128, 1)

    def split(row, mean):
        value, velocity = row, to_lane(row, -64)
        return (MEAN_FLOW * value if mean else 0.0) + velocity, value

    def derivative(own, before, after, width, coordinate, speed, mean):
        node = coordinate % 4
        flux, value = split(own, mean)
        out = 0.0
        for shift in range(-3, 4):
            weights = [table[n, n + shift] if 0 <= n + shift < 4 else 0.0 for n in range(4)]
            moved = flux if shift == 0 else to_lane(flux, -shift * width)
            out = out + by_node(node, weights) * moved
        sides = []
        for outside, end, step, back in ((after, 7, -width, 7 * width), (before, 0, width, -7 * width)):
            there_flux, there_value = split(outside, mean)
            at_end = coordinate == end
            sides.append((
                jnp.where(at_end, to_lane(there_flux, back), to_lane(flux, step)),
                jnp.where(at_end, to_lane(there_value, back), to_lane(value, step)),
            ))
        (up_flux, up_value), (low_flux, low_value) = sides
        up = 0.5 * (flux + up_flux) - 0.5 * speed * (up_value - value)
        low = 0.5 * (low_flux + flux) - 0.5 * speed * (value - low_value)
        out = out + jnp.where(node == 3, 6.0 * (up - flux), 0.0)
        return out - jnp.where(node == 0, 6.0 * (low - flux), 0.0)

    own = own_ref[0:4]
    change = derivative(own[0:1], before_x, after_x, 8, axial, 1.5, True)
    change = change + derivative(own[1:2], before_y, after_y, 1, azimuthal, 1.0, False)
    value, lower = own[0:1], own[2:3]
    radial = (
        np.float32(table[0, 0]) * value
        + np.float32(table[0, 1]) * to_lane(own[2:3], -64)
        + np.float32(table[0, 2]) * own[3:4]
        + np.float32(table[0, 3]) * to_lane(own[3:4], -64)
    )
    common = 0.5 * (lower + value) - 0.5 * (value - lower)
    change = change + (radial - 6.0 * (common - value))
    plane = jnp.where(point < 64, value - TIME_STEP * change, 0.0)
    terms = []
    for _ in range(3):
        term = plane.astype(jnp.bfloat16).astype(jnp.float32)
        terms.append(term)
        plane = plane - term
    rows = jnp.concatenate(terms + [jnp.zeros((5, 128), jnp.float32)], axis=0).astype(jnp.bfloat16)
    points = lax.broadcasted_iota(jnp.int32, (128, SLOTS), 0)
    index = index_ref[...].reshape(1, SLOTS)
    hit = jnp.where(index == points, 1.0, 0.0).astype(jnp.bfloat16)
    source = jnp.dot(rows, hit, preferred_element_type=jnp.float32)
    source = source[0:1] + source[1:2] + source[2:3]
    live = lax.broadcasted_iota(jnp.int32, (1, SLOTS), 1) < count_ref[0, 0]
    source_ref[...] = jnp.where(live, source, 0.0)


def neighbour(kind):
    moves = []
    for i in range(128):
        axial, azimuthal = i // 16, i % 16
        if kind == "core":
            axial ^= 1
        elif kind == "chip":
            axial = (axial + 1 if axial % 2 else axial - 1) % 8
        elif kind == "even":
            azimuthal ^= 1
        else:
            azimuthal = (azimuthal + 1 if azimuthal % 2 else azimuthal - 1) % 16
        moves.append((i, axial * 16 + azimuthal))
    return moves


def slot_source(tile, surf_index, surf_count):
    tiles = [
        lax.ppermute(tile, AXIAL + AZIMUTHAL, neighbour(kind)) for kind in ("core", "chip", "even", "odd")
    ]
    vmem = pl.BlockSpec(memory_space=pltpu.VMEM)
    smem = pl.BlockSpec(memory_space=pltpu.SMEM)
    return pl.pallas_call(
        source_kernel,
        in_specs=[vmem] * 6 + [smem],
        out_specs=vmem,
        out_shape=pltpu.VMEM((1, SLOTS), jnp.float32),
        compiler_params=pltpu.CompilerParams(vmem_limit_bytes=8 * 1024 * 1024),
        name="source",
    )(*in_vmem(tile, *tiles, surf_index), surf_count)


def bins_kernel(ahead, src_ref, src_b_ref, both_ref, out_ref, hi_s):
    own_ref, sib_ref = both_ref.at[0], both_ref.at[1]
    core = lax.axis_index("core")
    to = (here(0) + ahead) & 3
    base = to * jnp.where(core == 0, 256, 64)
    stride = jnp.where(core == 0, 64, 256)
    src = jnp.concatenate(
        [src_ref[:, :256], src_b_ref[:, :256], src_ref[:, 256:], src_b_ref[:, 256:],
         jnp.zeros((1, 96), jnp.float32)], axis=1)
    first16 = lax.broadcasted_iota(jnp.int32, (8, 128), 1) < 16
    row16 = lax.broadcasted_iota(jnp.int32, (16, LANES), 0)
    half = (row16 >= 8).astype(jnp.float32)
    count_lo = row16.astype(jnp.float32).astype(jnp.bfloat16)
    count_up = (row16 + 16).astype(jnp.float32).astype(jnp.bfloat16)
    one = jnp.ones((16, LANES), jnp.bfloat16)
    zero = jnp.zeros((16, LANES), jnp.bfloat16)
    lane = lax.broadcasted_iota(jnp.int32, (32, 128), 1) & 7
    lane8 = lax.broadcasted_iota(jnp.int32, (8, 128), 1) & 7
    diag8 = lane8 == lax.broadcasted_iota(jnp.int32, (8, 128), 0)

    def group(g, slot):
        row = base + (g // 8) * stride + (g % 8) * 8
        rows = pl.ds(pl.multiple_of(row, 8), 8)
        last, last_b = own_ref[rows, 512:], sib_ref[rows, 512:]
        last_k = jnp.where(first16, last, pltpu.roll(last_b, 16, 1))
        last_f = jnp.where(first16, pltpu.roll(last, 112, 1), last_b)
        k = jnp.concatenate([own_ref[rows, :256], sib_ref[rows, :256], last_k], axis=1)
        f = jnp.concatenate([own_ref[rows, 256:512], sib_ref[rows, 256:512], last_f], axis=1)
        c = src * (25.6 / (512.0 + k))
        up = f * c
        low = c - up
        hi = jnp.floor((k + 0.5) * (1.0 / 15.0))
        lo = k - 15.0 * hi
        hi_s[slot] = hi
        twice = lambda v: jnp.concatenate([v, v], axis=0)
        lo2 = (twice(lo) - half).astype(jnp.bfloat16)
        hi2 = (twice(hi) - half).astype(jnp.bfloat16)
        def parts(v):
            top = v.astype(jnp.bfloat16)
            rest = (v - top.astype(jnp.float32))
            return twice(v).astype(jnp.bfloat16), twice(rest).astype(jnp.bfloat16)
        low_a, low_b = parts(low)
        up_a, up_b = parts(up)
        wa, wb = [], []
        for j in range(0, 16, 2):
            at = lo2 == jnp.bfloat16(j)
            before = lo2 == jnp.bfloat16(j - 1)
            wa.append(jnp.where(at, low_a, jnp.where(before, up_a, zero)))
            wb.append(jnp.where(at, low_b, jnp.where(before, up_b, zero)))
        w = jnp.concatenate(wa + wb, axis=0)
        h = []
        for o in range(8):
            row = jnp.broadcast_to(hi_s[slot, o:o + 1, :], (16, LANES)).astype(jnp.bfloat16)
            h.append(jnp.where(row == count_lo, one, zero))
            h.append(jnp.where(row == count_up, one, zero))
        h.append(jnp.where(hi2 == jnp.bfloat16(32), one, zero))
        h.append(jnp.where(hi2 == jnp.bfloat16(34), one, zero))
        h = jnp.concatenate(h, axis=0)
        r = lax.dot_general(h, w, (((1,), (1,)), ((), ())), preferred_element_type=jnp.float32)
        r = r[:, :128] + r[:, 128:]
        main = r[0:32]
        for o in range(1, 8):
            main = jnp.where(lane == o, r[32 * o:32 * o + 32], main)
        extra = [jnp.sum(jnp.where(diag8, r[256 + 8 * e:264 + 8 * e], 0.0), axis=0, keepdims=True) for e in range(4)]
        return jnp.concatenate([main] + extra, axis=0)

    def several(p, _):
        for t in range(0, UNROLL, 2):
            g = UNROLL * p + t
            out_ref[g // 2] = jnp.concatenate([group(g, t), group(g + 1, t + 1)], axis=0)
        return 0

    lax.fori_loop(0, 32 // UNROLL, several, 0)


def bins(ahead, src, src_b, both):
    vmem = pl.BlockSpec(memory_space=pltpu.VMEM)
    return pl.pallas_call(
        functools.partial(bins_kernel, ahead),
        in_specs=[vmem] * 3,
        out_specs=vmem,
        scratch_shapes=[pltpu.VMEM((UNROLL, 8, LANES), jnp.float32)],
        out_shape=pltpu.VMEM((16, 2 * ROWS, 128), jnp.float32),
        compiler_params=pltpu.CompilerParams(vmem_limit_bytes=16 * 1024 * 1024),
        cost_estimate=pl.CostEstimate(
            flops=32 * 2 * 288 * 256 * LANES, bytes_accessed=8 * 256 * LANES, transcendentals=0
        ),
        name="bins",
    )(*in_vmem(src, src_b, both))


def keep_kernel(own_ref, sib_ref, to_ref, sems):
    copies = [
        pltpu.make_async_copy(array.at[pl.ds(128 * n, 128)], to_ref.at[k, pl.ds(128 * n, 128)], sems.at[k, n])
        for n in range(8)
        for k, array in enumerate((own_ref, sib_ref))
    ]
    for copy in copies:
        copy.start()
    for copy in copies:
        copy.wait()


def kept(own, sibling):
    return pl.pallas_call(
        keep_kernel,
        in_specs=[pl.BlockSpec(memory_space=pl.ANY)] * 2,
        out_specs=pl.BlockSpec(memory_space=pltpu.VMEM),
        out_shape=pltpu.VMEM((2,) + own.shape, own.dtype),
        scratch_shapes=[pltpu.SemaphoreType.DMA((2, 8))],
        compiler_params=pltpu.CompilerParams(vmem_limit_bytes=8 * 1024 * 1024),
        name="kept",
    )(own, sibling)


def shifted(array, phase, step):
    moves = []
    for i in range(128):
        at = {"x": i // 32, "core": i // 16 % 2, "y": i // 4 % 4, "z": i % 4}
        axis = ORDER[at["core"]][phase]
        at[axis] = (at[axis] + step) % 4
        moves.append((i, at["x"] * 32 + at["core"] * 16 + at["y"] * 4 + at["z"]))
    return lax.ppermute(array, AXIAL + AZIMUTHAL, moves)


def here(phase):
    return jnp.where(
        lax.axis_index("core") == 0, lax.axis_index(ORDER[0][phase]), lax.axis_index(ORDER[1][phase])
    )


def merge_kernel(phase, *refs):
    pieces, blocks = refs[:4], refs[4:]
    for block, step in zip(blocks, STEPS):
        at = (here(phase) + step) & 3
        block[...] = (pieces[0][at] + pieces[1][at]) + (pieces[2][at] + pieces[3][at])


def merged(pieces, phase):
    vmem = pl.BlockSpec(memory_space=pltpu.VMEM)
    return pl.pallas_call(
        functools.partial(merge_kernel, phase),
        in_specs=[vmem] * 4,
        out_specs=[vmem] * 4,
        out_shape=[pltpu.VMEM(pieces[0].shape[1:], jnp.float32)] * 4,
        compiler_params=pltpu.CompilerParams(vmem_limit_bytes=8 * 1024 * 1024),
        name="merged",
    )(*in_vmem(*pieces))


def summed(source, source_b, both):
    blocks = [bins(step, source, source_b, both) for step in STEPS]
    for phase in range(3):
        blocks = [shifted(block, phase, step) if step else block for block, step in zip(blocks, STEPS)]
        if phase < 2:
            blocks = merged([block.reshape((4, -1) + block.shape[-2:]) if block.shape[0] == 16 else block for block in blocks], phase + 1)
    return (blocks[0] + blocks[1]) + (blocks[2] + blocks[3])


def local(state, surf_index, surf_count, delay, fraction):
    core = lax.axis_index("core").reshape(1)
    swap = [(0, 1), (1, 0)]
    own, other, tile = first(core, state, delay, fraction)
    both = kept(own, lax.ppermute(other, "core", swap))
    source = slot_source(tile, surf_index, surf_count)
    source_b = lax.ppermute(source, "core", swap)
    total = summed(source, source_b, both)
    total = total.reshape(2, ROWS, 16, 8).transpose(0, 3, 1, 2).reshape(16, ROWS, 16)
    carry = jnp.pad(total[:, :34, 15:], ((0, 0), (1, 0), (0, 14)))
    return (total[:, :35, :RADIX] + carry).reshape(16, 35 * RADIX)[:, :SAMPLES]


def solution(mesh):
    fine = Mesh(mesh.devices.reshape(4, 2, 4, 4), ("x", "core", "y", "z"))
    ax, az = ("x", "core"), ("y", "z")
    placed = (
        P(None, ax, az, None),
        P(ax + az),
        P(ax, az),
        P(ax + az, None),
        P(ax + az, None),
    )
    return jax.shard_map(
        local, mesh=fine, in_specs=placed, out_specs=P(ax + az, None), check_vma=False
    )
```

```python
import functools

import jax
import jax.numpy as jnp
import numpy as np
from jax import lax
from jax.experimental import pallas as pl
from jax.experimental.pallas import tpu as pltpu
from jax.sharding import Mesh
from jax.sharding import PartitionSpec as P

SLOTS = 272
LANES = 640
RADIX = 15
ROWS = 36
STEPS = (2, 1, 3, 0)
SAMPLES = 512
ORDER = (("x", "y", "z"), ("y", "x", "z"))
AXIAL = ("x", "core")
AZIMUTHAL = ("y", "z")
MEAN_FLOW = 0.5
TIME_STEP = 0.05


def lobatto_matrix():
    points = np.array([-1.0, -1.0 / np.sqrt(5.0), 1.0 / np.sqrt(5.0), 1.0])
    table = np.zeros((4, 4))
    for i in range(4):
        for j in range(4):
            if i == j:
                table[i, j] = sum((1.0 / (points[i] - points[m]) for m in range(4) if m != i))
            else:
                a = np.prod([points[i] - points[m] for m in range(4) if m != i])
                b = np.prod([points[j] - points[m] for m in range(4) if m != j])
                table[i, j] = a / (b * (points[i] - points[j]))
    return table


def in_vmem(*arrays):
    return [pltpu.with_memory_space_constraint(array, pltpu.VMEM) for array in arrays]


def first_kernel(core_ref, state_ref, own_delay, own_fraction, other_delay, other_fraction, own_ref, other_ref, tile_ref):
    own_block = own_ref.at[pl.ds(pl.multiple_of(pl.program_id(0) * 256, 256), 256)]
    for delay, fraction, out in (
        (own_delay, own_fraction, own_block),
        (other_delay, other_fraction, other_ref),
    ):
        for at in (0, 128):
            rows = slice(at, at + 128)
            two = (delay[0:128, rows] + 512 * delay[128:256, rows]).astype(jnp.float32).T
            second = jnp.floor(two * (1.0 / 512.0))
            out[rows, 0:128] = two - 512.0 * second
            out[rows, 128:256] = second
            for base in (0, 128):
                out[rows, 256 + base : 384 + base] = fraction[base : base + 128, rows].T
            rest = [
                delay[256:272, rows].astype(jnp.float32),
                fraction[256:272, rows],
                jnp.zeros((96, 128), jnp.float32),
            ]
            out[rows, 512:640] = jnp.concatenate(rest, axis=0).T

    @pl.when(pl.program_id(0) == 0)
    def _():
        at = 4 * (state_ref.shape[2] // 8)
        value = state_ref[3] + state_ref[4]
        axial = jnp.concatenate([value, state_ref[1]], axis=0).T[at - 8 : at + 8]
        azimuthal = jnp.concatenate([value, state_ref[2]], axis=0).T[at : at + 8]
        first = lax.broadcasted_iota(jnp.int32, (1, 128), 1) < 64
        after = pltpu.roll(axial, 64, 1)
        rows = [
            axial[8:9],
            azimuthal[0:1],
            jnp.where(first, axial[7:8], after[9:10]),
            jnp.where(first, axial[10:11], after[11:12]),
            jnp.zeros((4, 128), jnp.float32),
        ]
        tile_ref[...] = jnp.concatenate(rows, axis=0)


def first(core, state, delay, fraction):
    mine = pl.BlockSpec((SLOTS, 256), lambda n, c: (0, 2 * n + c[0]))
    other = pl.BlockSpec((SLOTS, 256), lambda n, c: (0, 2 * n + 1 - c[0]))
    state = state.reshape(5, 64, state.shape[3])
    delay, fraction, state = (
        pltpu.with_memory_space_constraint(array, pltpu.HBM) for array in (delay, fraction, state)
    )
    return pl.pallas_call(
        first_kernel,
        grid_spec=pltpu.PrefetchScalarGridSpec(
            num_scalar_prefetch=1,
            grid=(4,),
            in_specs=[pl.BlockSpec(state.shape, lambda n, c: (0, 0, 0)), mine, mine, other, other],
            out_specs=[
                pl.BlockSpec(memory_space=pltpu.VMEM),
                pl.BlockSpec((256, LANES), lambda n, c: (n, 0)),
                pl.BlockSpec((8, 128), lambda n, c: (0, 0)),
            ],
        ),
        out_shape=[
            pltpu.VMEM((1024, LANES), jnp.float32),
            jax.ShapeDtypeStruct((1024, LANES), jnp.float32),
            pltpu.VMEM((8, 128), jnp.float32),
        ],
        compiler_params=pltpu.CompilerParams(vmem_limit_bytes=16 * 1024 * 1024),
        name="first",
    )(core, state, delay, fraction, delay, fraction)


def by_node(node, values):
    out = jnp.full(node.shape, values[0], jnp.float32)
    for n in (1, 2, 3):
        out = jnp.where(node == n, jnp.float32(values[n]), out)
    return out


def source_kernel(own_ref, core_ref, chip_ref, even_ref, odd_ref, index_ref, count_ref, source_ref):
    table = lobatto_matrix()
    point = lax.broadcasted_iota(jnp.int32, (1, 128), 1)
    axial, azimuthal = point // 8, point % 8
    x, core = lax.axis_index("x"), lax.axis_index("core")
    second = core == 1
    odd = lax.rem(lax.axis_index("z"), 2) == 1
    no_before, no_after = x * 2 + core == 0, x * 2 + core == 7
    core_tile, chip = core_ref[...], chip_ref[...]
    before_x = jnp.where(no_before, 0.0, jnp.where(second, core_tile, chip))[0:1]
    after_x = jnp.where(no_after, 0.0, jnp.where(second, chip, core_tile))[0:1]
    even, odd_tile = even_ref[...], odd_ref[...]
    before_y = jnp.where(odd, even, odd_tile)[1:2]
    after_y = jnp.where(odd, odd_tile, even)[1:2]

    def to_lane(array, shift):
        return pltpu.roll(array, shift % 128, 1)

    def split(row, mean):
        value, velocity = row, to_lane(row, -64)
        return (MEAN_FLOW * value if mean else 0.0) + velocity, value

    def derivative(own, before, after, width, coordinate, speed, mean):
        node = coordinate % 4
        flux, value = split(own, mean)
        out = 0.0
        for shift in range(-3, 4):
            weights = [table[n, n + shift] if 0 <= n + shift < 4 else 0.0 for n in range(4)]
            moved = flux if shift == 0 else to_lane(flux, -shift * width)
            out = out + by_node(node, weights) * moved
        sides = []
        for outside, end, step, back in ((after, 7, -width, 7 * width), (before, 0, width, -7 * width)):
            there_flux, there_value = split(outside, mean)
            at_end = coordinate == end
            sides.append((
                jnp.where(at_end, to_lane(there_flux, back), to_lane(flux, step)),
                jnp.where(at_end, to_lane(there_value, back), to_lane(value, step)),
            ))
        (up_flux, up_value), (low_flux, low_value) = sides
        up = 0.5 * (flux + up_flux) - 0.5 * speed * (up_value - value)
        low = 0.5 * (low_flux + flux) - 0.5 * speed * (value - low_value)
        out = out + jnp.where(node == 3, 6.0 * (up - flux), 0.0)
        return out - jnp.where(node == 0, 6.0 * (low - flux), 0.0)

    own = own_ref[0:4]
    change = derivative(own[0:1], before_x, after_x, 8, axial, 1.5, True)
    change = change + derivative(own[1:2], before_y, after_y, 1, azimuthal, 1.0, False)
    value, lower = own[0:1], own[2:3]
    radial = (
        np.float32(table[0, 0]) * value
        + np.float32(table[0, 1]) * to_lane(own[2:3], -64)
        + np.float32(table[0, 2]) * own[3:4]
        + np.float32(table[0, 3]) * to_lane(own[3:4], -64)
    )
    common = 0.5 * (lower + value) - 0.5 * (value - lower)
    change = change + (radial - 6.0 * (common - value))
    plane = jnp.where(point < 64, value - TIME_STEP * change, 0.0)
    terms = []
    for _ in range(3):
        term = plane.astype(jnp.bfloat16).astype(jnp.float32)
        terms.append(term)
        plane = plane - term
    rows = jnp.concatenate(terms + [jnp.zeros((5, 128), jnp.float32)], axis=0).astype(jnp.bfloat16)
    points = lax.broadcasted_iota(jnp.int32, (128, SLOTS), 0)
    index = index_ref[...].reshape(1, SLOTS)
    hit = jnp.where(index == points, 1.0, 0.0).astype(jnp.bfloat16)
    source = jnp.dot(rows, hit, preferred_element_type=jnp.float32)
    source = source[0:1] + source[1:2] + source[2:3]
    live = lax.broadcasted_iota(jnp.int32, (1, SLOTS), 1) < count_ref[0, 0]
    source_ref[...] = jnp.where(live, source, 0.0)


def neighbour(kind):
    moves = []
    for i in range(128):
        axial, azimuthal = i // 16, i % 16
        if kind == "core":
            axial ^= 1
        elif kind == "chip":
            axial = (axial + 1 if axial % 2 else axial - 1) % 8
        elif kind == "even":
            azimuthal ^= 1
        else:
            azimuthal = (azimuthal + 1 if azimuthal % 2 else azimuthal - 1) % 16
        moves.append((i, axial * 16 + azimuthal))
    return moves


def slot_source(tile, surf_index, surf_count):
    tiles = [
        lax.ppermute(tile, AXIAL + AZIMUTHAL, neighbour(kind)) for kind in ("core", "chip", "even", "odd")
    ]
    vmem = pl.BlockSpec(memory_space=pltpu.VMEM)
    smem = pl.BlockSpec(memory_space=pltpu.SMEM)
    return pl.pallas_call(
        source_kernel,
        in_specs=[vmem] * 6 + [smem],
        out_specs=vmem,
        out_shape=pltpu.VMEM((1, SLOTS), jnp.float32),
        compiler_params=pltpu.CompilerParams(vmem_limit_bytes=8 * 1024 * 1024),
        name="source",
    )(*in_vmem(tile, *tiles, surf_index), surf_count)


def bins_kernel(ahead, start, count, src_ref, src_b_ref, own_ref, sib_ref, out_ref, hi_s):
    core = lax.axis_index("core")
    to = (here(0) + ahead) & 3
    base = to * jnp.where(core == 0, 256, 64)
    stride = jnp.where(core == 0, 64, 256)
    src = jnp.concatenate(
        [src_ref[:, :256], src_b_ref[:, :256], src_ref[:, 256:], src_b_ref[:, 256:],
         jnp.zeros((1, 96), jnp.float32)], axis=1)
    first16 = lax.broadcasted_iota(jnp.int32, (8, 128), 1) < 16
    row16 = lax.broadcasted_iota(jnp.int32, (16, LANES), 0)
    half = (row16 >= 8).astype(jnp.float32)
    count_lo = row16.astype(jnp.float32).astype(jnp.bfloat16)
    count_up = (row16 + 16).astype(jnp.float32).astype(jnp.bfloat16)
    one = jnp.ones((16, LANES), jnp.bfloat16)
    zero = jnp.zeros((16, LANES), jnp.bfloat16)
    lane = lax.broadcasted_iota(jnp.int32, (32, 128), 1) & 7
    lane8 = lax.broadcasted_iota(jnp.int32, (8, 128), 1) & 7
    diag8 = lane8 == lax.broadcasted_iota(jnp.int32, (8, 128), 0)

    def group(g, slot):
        row = base + (g // 8) * stride + (g % 8) * 8
        rows = pl.ds(pl.multiple_of(row, 8), 8)
        last, last_b = own_ref[rows, 512:], sib_ref[rows, 512:]
        last_k = jnp.where(first16, last, pltpu.roll(last_b, 16, 1))
        last_f = jnp.where(first16, pltpu.roll(last, 112, 1), last_b)
        k = jnp.concatenate([own_ref[rows, :256], sib_ref[rows, :256], last_k], axis=1)
        f = jnp.concatenate([own_ref[rows, 256:512], sib_ref[rows, 256:512], last_f], axis=1)
        c = src * (25.6 / (512.0 + k))
        up = f * c
        low = c - up
        hi = jnp.floor((k + 0.5) * (1.0 / 15.0))
        lo = k - 15.0 * hi
        hi_s[slot] = hi
        twice = lambda v: jnp.concatenate([v, v], axis=0)
        lo2 = (twice(lo) - half).astype(jnp.bfloat16)
        hi2 = (twice(hi) - half).astype(jnp.bfloat16)
        def parts(v):
            top = v.astype(jnp.bfloat16)
            rest = (v - top.astype(jnp.float32))
            return twice(v).astype(jnp.bfloat16), twice(rest).astype(jnp.bfloat16)
        low_a, low_b = parts(low)
        up_a, up_b = parts(up)
        wa, wb = [], []
        for j in range(0, 16, 2):
            at = lo2 == jnp.bfloat16(j)
            before = lo2 == jnp.bfloat16(j - 1)
            wa.append(jnp.where(at, low_a, jnp.where(before, up_a, zero)))
            wb.append(jnp.where(at, low_b, jnp.where(before, up_b, zero)))
        w = jnp.concatenate(wa + wb, axis=0)
        h = []
        for o in range(8):
            row = jnp.broadcast_to(hi_s[slot, o:o + 1, :], (16, LANES)).astype(jnp.bfloat16)
            h.append(jnp.where(row == count_lo, one, zero))
            h.append(jnp.where(row == count_up, one, zero))
        h.append(jnp.where(hi2 == jnp.bfloat16(32), one, zero))
        h.append(jnp.where(hi2 == jnp.bfloat16(34), one, zero))
        h = jnp.concatenate(h, axis=0)
        r = lax.dot_general(h, w, (((1,), (1,)), ((), ())), preferred_element_type=jnp.float32)
        r = r[:, :128] + r[:, 128:]
        main = r[0:32]
        for o in range(1, 8):
            main = jnp.where(lane == o, r[32 * o:32 * o + 32], main)
        extra = [jnp.sum(jnp.where(diag8, r[256 + 8 * e:264 + 8 * e], 0.0), axis=0, keepdims=True) for e in range(4)]
        return jnp.concatenate([main] + extra, axis=0)

    for t in range(0, count, 2):
        out_ref[t // 2] = jnp.concatenate([group(start + t, t), group(start + t + 1, t + 1)], axis=0)


def bins(ahead, half, src, src_b, own, sibling):
    vmem = pl.BlockSpec(memory_space=pltpu.VMEM)
    start, count = (0, 32) if half is None else (16 * half, 16)
    return pl.pallas_call(
        functools.partial(bins_kernel, ahead, start, count),
        in_specs=[vmem] * 4,
        out_specs=vmem,
        scratch_shapes=[pltpu.VMEM((count, 8, LANES), jnp.float32)],
        out_shape=pltpu.VMEM((count // 2, 2 * ROWS, 128), jnp.float32),
        compiler_params=pltpu.CompilerParams(vmem_limit_bytes=16 * 1024 * 1024),
        cost_estimate=pl.CostEstimate(
            flops=32 * 2 * 288 * 256 * LANES, bytes_accessed=8 * 256 * LANES, transcendentals=0
        ),
        name="bins",
    )(*in_vmem(src, src_b, own, sibling))


def keep_kernel(from_ref, to_ref, sems):
    rows = [pl.ds(128 * n, 128) for n in range(8)]
    copies = [pltpu.make_async_copy(from_ref.at[r], to_ref.at[r], sems.at[n]) for n, r in enumerate(rows)]
    for copy in copies:
        copy.start()
    for copy in copies:
        copy.wait()


def kept(array):
    return pl.pallas_call(
        keep_kernel,
        in_specs=[pl.BlockSpec(memory_space=pl.ANY)],
        out_specs=pl.BlockSpec(memory_space=pltpu.VMEM),
        out_shape=pltpu.VMEM(array.shape, array.dtype),
        scratch_shapes=[pltpu.SemaphoreType.DMA((8,))],
        compiler_params=pltpu.CompilerParams(vmem_limit_bytes=8 * 1024 * 1024),
        name="kept",
    )(array)


def shifted(array, phase, step):
    moves = []
    for i in range(128):
        at = {"x": i // 32, "core": i // 16 % 2, "y": i // 4 % 4, "z": i % 4}
        axis = ORDER[at["core"]][phase]
        at[axis] = (at[axis] + step) % 4
        moves.append((i, at["x"] * 32 + at["core"] * 16 + at["y"] * 4 + at["z"]))
    return lax.ppermute(array, AXIAL + AZIMUTHAL, moves)


def here(phase):
    return jnp.where(
        lax.axis_index("core") == 0, lax.axis_index(ORDER[0][phase]), lax.axis_index(ORDER[1][phase])
    )


def merge_kernel(phase, *refs):
    pieces, blocks = refs[:-4], refs[-4:]
    for block, step in zip(blocks, STEPS):
        at = (here(phase) + step) & 3
        total = pieces[0][at] + pieces[1][at] + pieces[-1][at]
        if len(pieces) == 4:
            block[...] = total + pieces[2][at]
        else:
            block[...] = total + jnp.where(at < 2, pieces[2][at & 1], pieces[3][at & 1])


def merged(pieces, phase):
    vmem = pl.BlockSpec(memory_space=pltpu.VMEM)
    return pl.pallas_call(
        functools.partial(merge_kernel, phase),
        in_specs=[vmem] * len(pieces),
        out_specs=[vmem] * 4,
        out_shape=[pltpu.VMEM(pieces[0].shape[1:], jnp.float32)] * 4,
        compiler_params=pltpu.CompilerParams(vmem_limit_bytes=8 * 1024 * 1024),
        name="merged",
    )(*in_vmem(*pieces))


def summed(source, source_b, own, sibling):
    operands = (source, source_b, own, sibling)
    parts = [(2, None), (1, None), (3, 0), (3, 1), (0, None)]
    pieces = [bins(step, half, *operands) for step, half in parts]
    pieces = [shifted(piece, 0, step) if step else piece for piece, (step, _) in zip(pieces, parts)]
    blocks = merged([piece.reshape(-1, 4, 2 * ROWS, 128) for piece in pieces], 1)
    for phase in (1, 2):
        blocks = [shifted(block, phase, step) if step else block for block, step in zip(blocks, STEPS)]
        if phase == 1:
            blocks = merged(blocks, 2)
    return (blocks[0] + blocks[1]) + (blocks[2] + blocks[3])


def local(state, surf_index, surf_count, delay, fraction):
    core = lax.axis_index("core").reshape(1)
    swap = [(0, 1), (1, 0)]
    own, other, tile = first(core, state, delay, fraction)
    sibling = kept(lax.ppermute(other, "core", swap))
    source = slot_source(tile, surf_index, surf_count)
    source_b = lax.ppermute(source, "core", swap)
    total = summed(source, source_b, own, sibling)
    total = total.reshape(2, ROWS, 16, 8).transpose(0, 3, 1, 2).reshape(16, ROWS, 16)
    carry = jnp.pad(total[:, :34, 15:], ((0, 0), (1, 0), (0, 14)))
    return (total[:, :35, :RADIX] + carry).reshape(16, 35 * RADIX)[:, :SAMPLES]


def solution(mesh):
    fine = Mesh(mesh.devices.reshape(4, 2, 4, 4), ("x", "core", "y", "z"))
    ax, az = ("x", "core"), ("y", "z")
    placed = (
        P(None, ax, az, None),
        P(ax + az),
        P(ax, az),
        P(ax + az, None),
        P(ax + az, None),
    )
    return jax.shard_map(
        local, mesh=fine, in_specs=placed, out_specs=P(ax + az, None), check_vma=False
    )
```

```python
import functools

import jax
import jax.numpy as jnp
import numpy as np
from jax import lax
from jax.experimental import pallas as pl
from jax.experimental.pallas import tpu as pltpu
from jax.sharding import Mesh
from jax.sharding import PartitionSpec as P

SLOTS = 272
LANES = 640
RADIX = 15
ROWS = 36
STEPS = (2, 1, 3, 0)
SAMPLES = 512
ORDER = (("x", "y", "z"), ("y", "x", "z"))
AXIAL = ("x", "core")
AZIMUTHAL = ("y", "z")
MEAN_FLOW = 0.5
TIME_STEP = 0.05


def lobatto_matrix():
    points = np.array([-1.0, -1.0 / np.sqrt(5.0), 1.0 / np.sqrt(5.0), 1.0])
    table = np.zeros((4, 4))
    for i in range(4):
        for j in range(4):
            if i == j:
                table[i, j] = sum((1.0 / (points[i] - points[m]) for m in range(4) if m != i))
            else:
                a = np.prod([points[i] - points[m] for m in range(4) if m != i])
                b = np.prod([points[j] - points[m] for m in range(4) if m != j])
                table[i, j] = a / (b * (points[i] - points[j]))
    return table


def in_vmem(*arrays):
    return [pltpu.with_memory_space_constraint(array, pltpu.VMEM) for array in arrays]


def first_kernel(core_ref, state_ref, own_delay, own_fraction, other_delay, other_fraction, own_ref, other_ref, tile_ref):
    own_block = own_ref.at[pl.ds(pl.multiple_of(pl.program_id(0) * 128, 128), 128)]
    for delay, fraction, out in (
        (own_delay, own_fraction, own_block),
        (other_delay, other_fraction, other_ref),
    ):
        for rows in (slice(0, 128),):
            two = (delay[0:128, rows] + 512 * delay[128:256, rows]).astype(jnp.float32).T
            second = jnp.floor(two * (1.0 / 512.0))
            out[rows, 0:128] = two - 512.0 * second
            out[rows, 128:256] = second
            for base in (0, 128):
                out[rows, 256 + base : 384 + base] = fraction[base : base + 128, rows].T
            rest = [
                delay[256:272, rows].astype(jnp.float32),
                fraction[256:272, rows],
                jnp.zeros((96, 128), jnp.float32),
            ]
            out[rows, 512:640] = jnp.concatenate(rest, axis=0).T

    @pl.when(pl.program_id(0) == 0)
    def _():
        at = 4 * (state_ref.shape[2] // 8)
        value = state_ref[3] + state_ref[4]
        axial = jnp.concatenate([value, state_ref[1]], axis=0).T[at - 8 : at + 8]
        azimuthal = jnp.concatenate([value, state_ref[2]], axis=0).T[at : at + 8]
        first = lax.broadcasted_iota(jnp.int32, (1, 128), 1) < 64
        after = pltpu.roll(axial, 64, 1)
        rows = [
            axial[8:9],
            azimuthal[0:1],
            jnp.where(first, axial[7:8], after[9:10]),
            jnp.where(first, axial[10:11], after[11:12]),
            jnp.zeros((4, 128), jnp.float32),
        ]
        tile_ref[...] = jnp.concatenate(rows, axis=0)


def first(core, state, delay, fraction):
    mine = pl.BlockSpec((SLOTS, 128), lambda n, c: (0, n // 2 * 4 + 2 * c[0] + n % 2))
    other = pl.BlockSpec((SLOTS, 128), lambda n, c: (0, n // 2 * 4 + 2 - 2 * c[0] + n % 2))
    state = state.reshape(5, 64, state.shape[3])
    delay, fraction, state = (
        pltpu.with_memory_space_constraint(array, pltpu.HBM) for array in (delay, fraction, state)
    )
    return pl.pallas_call(
        first_kernel,
        grid_spec=pltpu.PrefetchScalarGridSpec(
            num_scalar_prefetch=1,
            grid=(8,),
            in_specs=[pl.BlockSpec(state.shape, lambda n, c: (0, 0, 0)), mine, mine, other, other],
            out_specs=[
                pl.BlockSpec(memory_space=pltpu.VMEM),
                pl.BlockSpec((128, LANES), lambda n, c: (n, 0)),
                pl.BlockSpec((8, 128), lambda n, c: (0, 0)),
            ],
        ),
        out_shape=[
            pltpu.VMEM((1024, LANES), jnp.float32),
            jax.ShapeDtypeStruct((1024, LANES), jnp.float32),
            pltpu.VMEM((8, 128), jnp.float32),
        ],
        compiler_params=pltpu.CompilerParams(vmem_limit_bytes=16 * 1024 * 1024),
        name="first",
    )(core, state, delay, fraction, delay, fraction)


def by_node(node, values):
    out = jnp.full(node.shape, values[0], jnp.float32)
    for n in (1, 2, 3):
        out = jnp.where(node == n, jnp.float32(values[n]), out)
    return out


def source_kernel(own_ref, core_ref, chip_ref, even_ref, odd_ref, index_ref, count_ref, source_ref):
    table = lobatto_matrix()
    point = lax.broadcasted_iota(jnp.int32, (1, 128), 1)
    axial, azimuthal = point // 8, point % 8
    x, core = lax.axis_index("x"), lax.axis_index("core")
    second = core == 1
    odd = lax.rem(lax.axis_index("z"), 2) == 1
    no_before, no_after = x * 2 + core == 0, x * 2 + core == 7
    core_tile, chip = core_ref[...], chip_ref[...]
    before_x = jnp.where(no_before, 0.0, jnp.where(second, core_tile, chip))[0:1]
    after_x = jnp.where(no_after, 0.0, jnp.where(second, chip, core_tile))[0:1]
    even, odd_tile = even_ref[...], odd_ref[...]
    before_y = jnp.where(odd, even, odd_tile)[1:2]
    after_y = jnp.where(odd, odd_tile, even)[1:2]

    def to_lane(array, shift):
        return pltpu.roll(array, shift % 128, 1)

    def split(row, mean):
        value, velocity = row, to_lane(row, -64)
        return (MEAN_FLOW * value if mean else 0.0) + velocity, value

    def derivative(own, before, after, width, coordinate, speed, mean):
        node = coordinate % 4
        flux, value = split(own, mean)
        out = 0.0
        for shift in range(-3, 4):
            weights = [table[n, n + shift] if 0 <= n + shift < 4 else 0.0 for n in range(4)]
            moved = flux if shift == 0 else to_lane(flux, -shift * width)
            out = out + by_node(node, weights) * moved
        sides = []
        for outside, end, step, back in ((after, 7, -width, 7 * width), (before, 0, width, -7 * width)):
            there_flux, there_value = split(outside, mean)
            at_end = coordinate == end
            sides.append((
                jnp.where(at_end, to_lane(there_flux, back), to_lane(flux, step)),
                jnp.where(at_end, to_lane(there_value, back), to_lane(value, step)),
            ))
        (up_flux, up_value), (low_flux, low_value) = sides
        up = 0.5 * (flux + up_flux) - 0.5 * speed * (up_value - value)
        low = 0.5 * (low_flux + flux) - 0.5 * speed * (value - low_value)
        out = out + jnp.where(node == 3, 6.0 * (up - flux), 0.0)
        return out - jnp.where(node == 0, 6.0 * (low - flux), 0.0)

    own = own_ref[0:4]
    change = derivative(own[0:1], before_x, after_x, 8, axial, 1.5, True)
    change = change + derivative(own[1:2], before_y, after_y, 1, azimuthal, 1.0, False)
    value, lower = own[0:1], own[2:3]
    radial = (
        np.float32(table[0, 0]) * value
        + np.float32(table[0, 1]) * to_lane(own[2:3], -64)
        + np.float32(table[0, 2]) * own[3:4]
        + np.float32(table[0, 3]) * to_lane(own[3:4], -64)
    )
    common = 0.5 * (lower + value) - 0.5 * (value - lower)
    change = change + (radial - 6.0 * (common - value))
    plane = jnp.where(point < 64, value - TIME_STEP * change, 0.0)
    terms = []
    for _ in range(3):
        term = plane.astype(jnp.bfloat16).astype(jnp.float32)
        terms.append(term)
        plane = plane - term
    rows = jnp.concatenate(terms + [jnp.zeros((5, 128), jnp.float32)], axis=0).astype(jnp.bfloat16)
    points = lax.broadcasted_iota(jnp.int32, (128, SLOTS), 0)
    index = index_ref[...].reshape(1, SLOTS)
    hit = jnp.where(index == points, 1.0, 0.0).astype(jnp.bfloat16)
    source = jnp.dot(rows, hit, preferred_element_type=jnp.float32)
    source = source[0:1] + source[1:2] + source[2:3]
    live = lax.broadcasted_iota(jnp.int32, (1, SLOTS), 1) < count_ref[0, 0]
    source_ref[...] = jnp.where(live, source, 0.0)


def neighbour(kind):
    moves = []
    for i in range(128):
        axial, azimuthal = i // 16, i % 16
        if kind == "core":
            axial ^= 1
        elif kind == "chip":
            axial = (axial + 1 if axial % 2 else axial - 1) % 8
        elif kind == "even":
            azimuthal ^= 1
        else:
            azimuthal = (azimuthal + 1 if azimuthal % 2 else azimuthal - 1) % 16
        moves.append((i, axial * 16 + azimuthal))
    return moves


def slot_source(tile, surf_index, surf_count):
    tiles = [
        lax.ppermute(tile, AXIAL + AZIMUTHAL, neighbour(kind)) for kind in ("core", "chip", "even", "odd")
    ]
    vmem = pl.BlockSpec(memory_space=pltpu.VMEM)
    smem = pl.BlockSpec(memory_space=pltpu.SMEM)
    return pl.pallas_call(
        source_kernel,
        in_specs=[vmem] * 6 + [smem],
        out_specs=vmem,
        out_shape=pltpu.VMEM((1, SLOTS), jnp.float32),
        compiler_params=pltpu.CompilerParams(vmem_limit_bytes=8 * 1024 * 1024),
        name="source",
    )(*in_vmem(tile, *tiles, surf_index), surf_count)


def bins_kernel(ahead, start, count, src_ref, src_b_ref, own_ref, sib_ref, out_ref, hi_s):
    core = lax.axis_index("core")
    to = (here(0) + ahead) & 3
    base = to * jnp.where(core == 0, 256, 64)
    stride = jnp.where(core == 0, 64, 256)
    src = jnp.concatenate(
        [src_ref[:, :256], src_b_ref[:, :256], src_ref[:, 256:], src_b_ref[:, 256:],
         jnp.zeros((1, 96), jnp.float32)], axis=1)
    first16 = lax.broadcasted_iota(jnp.int32, (8, 128), 1) < 16
    row16 = lax.broadcasted_iota(jnp.int32, (16, LANES), 0)
    half = (row16 >= 8).astype(jnp.float32)
    count_lo = row16.astype(jnp.float32).astype(jnp.bfloat16)
    count_up = (row16 + 16).astype(jnp.float32).astype(jnp.bfloat16)
    one = jnp.ones((16, LANES), jnp.bfloat16)
    zero = jnp.zeros((16, LANES), jnp.bfloat16)
    lane = lax.broadcasted_iota(jnp.int32, (32, 128), 1) & 7
    lane8 = lax.broadcasted_iota(jnp.int32, (8, 128), 1) & 7
    diag8 = lane8 == lax.broadcasted_iota(jnp.int32, (8, 128), 0)

    def group(g, slot):
        row = base + (g // 8) * stride + (g % 8) * 8
        rows = pl.ds(pl.multiple_of(row, 8), 8)
        last, last_b = own_ref[rows, 512:], sib_ref[rows, 512:]
        last_k = jnp.where(first16, last, pltpu.roll(last_b, 16, 1))
        last_f = jnp.where(first16, pltpu.roll(last, 112, 1), last_b)
        k = jnp.concatenate([own_ref[rows, :256], sib_ref[rows, :256], last_k], axis=1)
        f = jnp.concatenate([own_ref[rows, 256:512], sib_ref[rows, 256:512], last_f], axis=1)
        c = src * (25.6 / (512.0 + k))
        up = f * c
        low = c - up
        hi = jnp.floor((k + 0.5) * (1.0 / 15.0))
        lo = k - 15.0 * hi
        hi_s[slot] = hi
        twice = lambda v: jnp.concatenate([v, v], axis=0)
        lo2 = (twice(lo) - half).astype(jnp.bfloat16)
        hi2 = (twice(hi) - half).astype(jnp.bfloat16)
        def parts(v):
            top = v.astype(jnp.bfloat16)
            rest = (v - top.astype(jnp.float32))
            return twice(v).astype(jnp.bfloat16), twice(rest).astype(jnp.bfloat16)
        low_a, low_b = parts(low)
        up_a, up_b = parts(up)
        wa, wb = [], []
        for j in range(0, 16, 2):
            at = lo2 == jnp.bfloat16(j)
            before = lo2 == jnp.bfloat16(j - 1)
            wa.append(jnp.where(at, low_a, jnp.where(before, up_a, zero)))
            wb.append(jnp.where(at, low_b, jnp.where(before, up_b, zero)))
        w = jnp.concatenate(wa + wb, axis=0)
        h = []
        for o in range(8):
            row = jnp.broadcast_to(hi_s[slot, o:o + 1, :], (16, LANES)).astype(jnp.bfloat16)
            h.append(jnp.where(row == count_lo, one, zero))
            h.append(jnp.where(row == count_up, one, zero))
        h.append(jnp.where(hi2 == jnp.bfloat16(32), one, zero))
        h.append(jnp.where(hi2 == jnp.bfloat16(34), one, zero))
        h = jnp.concatenate(h, axis=0)
        r = lax.dot_general(h, w, (((1,), (1,)), ((), ())), preferred_element_type=jnp.float32)
        r = r[:, :128] + r[:, 128:]
        main = r[0:32]
        for o in range(1, 8):
            main = jnp.where(lane == o, r[32 * o:32 * o + 32], main)
        extra = [jnp.sum(jnp.where(diag8, r[256 + 8 * e:264 + 8 * e], 0.0), axis=0, keepdims=True) for e in range(4)]
        return jnp.concatenate([main] + extra, axis=0)

    for t in range(0, count, 2):
        out_ref[t // 2] = jnp.concatenate([group(start + t, t), group(start + t + 1, t + 1)], axis=0)


def bins(ahead, half, src, src_b, own, sibling):
    vmem = pl.BlockSpec(memory_space=pltpu.VMEM)
    start, count = (0, 32) if half is None else (16 * half, 16)
    return pl.pallas_call(
        functools.partial(bins_kernel, ahead, start, count),
        in_specs=[vmem] * 4,
        out_specs=vmem,
        scratch_shapes=[pltpu.VMEM((count, 8, LANES), jnp.float32)],
        out_shape=pltpu.VMEM((count // 2, 2 * ROWS, 128), jnp.float32),
        compiler_params=pltpu.CompilerParams(vmem_limit_bytes=16 * 1024 * 1024),
        cost_estimate=pl.CostEstimate(
            flops=32 * 2 * 288 * 256 * LANES, bytes_accessed=8 * 256 * LANES, transcendentals=0
        ),
        name="bins",
    )(*in_vmem(src, src_b, own, sibling))


def keep_kernel(from_ref, to_ref, sems):
    rows = [pl.ds(128 * n, 128) for n in range(8)]
    copies = [pltpu.make_async_copy(from_ref.at[r], to_ref.at[r], sems.at[n]) for n, r in enumerate(rows)]
    for copy in copies:
        copy.start()
    for copy in copies:
        copy.wait()


def kept(array):
    return pl.pallas_call(
        keep_kernel,
        in_specs=[pl.BlockSpec(memory_space=pl.ANY)],
        out_specs=pl.BlockSpec(memory_space=pltpu.VMEM),
        out_shape=pltpu.VMEM(array.shape, array.dtype),
        scratch_shapes=[pltpu.SemaphoreType.DMA((8,))],
        compiler_params=pltpu.CompilerParams(vmem_limit_bytes=8 * 1024 * 1024),
        name="kept",
    )(array)


def shifted(array, phase, step):
    moves = []
    for i in range(128):
        at = {"x": i // 32, "core": i // 16 % 2, "y": i // 4 % 4, "z": i % 4}
        axis = ORDER[at["core"]][phase]
        at[axis] = (at[axis] + step) % 4
        moves.append((i, at["x"] * 32 + at["core"] * 16 + at["y"] * 4 + at["z"]))
    return lax.ppermute(array, AXIAL + AZIMUTHAL, moves)


def here(phase):
    return jnp.where(
        lax.axis_index("core") == 0, lax.axis_index(ORDER[0][phase]), lax.axis_index(ORDER[1][phase])
    )


def merge_kernel(phase, *refs):
    pieces, blocks = refs[:-4], refs[-4:]
    for block, step in zip(blocks, STEPS):
        at = (here(phase) + step) & 3
        total = pieces[0][at] + pieces[1][at] + pieces[-1][at]
        if len(pieces) == 4:
            block[...] = total + pieces[2][at]
        else:
            block[...] = total + jnp.where(at < 2, pieces[2][at & 1], pieces[3][at & 1])


def merged(pieces, phase):
    vmem = pl.BlockSpec(memory_space=pltpu.VMEM)
    return pl.pallas_call(
        functools.partial(merge_kernel, phase),
        in_specs=[vmem] * len(pieces),
        out_specs=[vmem] * 4,
        out_shape=[pltpu.VMEM(pieces[0].shape[1:], jnp.float32)] * 4,
        compiler_params=pltpu.CompilerParams(vmem_limit_bytes=8 * 1024 * 1024),
        name="merged",
    )(*in_vmem(*pieces))


def summed(source, source_b, own, sibling):
    operands = (source, source_b, own, sibling)
    parts = [(2, None), (1, None), (3, 0), (3, 1), (0, None)]
    pieces = [bins(step, half, *operands) for step, half in parts]
    pieces = [shifted(piece, 0, step) if step else piece for piece, (step, _) in zip(pieces, parts)]
    blocks = merged([piece.reshape(-1, 4, 2 * ROWS, 128) for piece in pieces], 1)
    for phase in (1, 2):
        blocks = [shifted(block, phase, step) if step else block for block, step in zip(blocks, STEPS)]
        if phase == 1:
            blocks = merged(blocks, 2)
    return (blocks[0] + blocks[1]) + (blocks[2] + blocks[3])


def local(state, surf_index, surf_count, delay, fraction):
    core = lax.axis_index("core").reshape(1)
    swap = [(0, 1), (1, 0)]
    own, other, tile = first(core, state, delay, fraction)
    sibling = kept(lax.ppermute(other, "core", swap))
    source = slot_source(tile, surf_index, surf_count)
    source_b = lax.ppermute(source, "core", swap)
    total = summed(source, source_b, own, sibling)
    total = total.reshape(2, ROWS, 16, 8).transpose(0, 3, 1, 2).reshape(16, ROWS, 16)
    carry = jnp.pad(total[:, :34, 15:], ((0, 0), (1, 0), (0, 14)))
    return (total[:, :35, :RADIX] + carry).reshape(16, 35 * RADIX)[:, :SAMPLES]


def solution(mesh):
    fine = Mesh(mesh.devices.reshape(4, 2, 4, 4), ("x", "core", "y", "z"))
    ax, az = ("x", "core"), ("y", "z")
    placed = (
        P(None, ax, az, None),
        P(ax + az),
        P(ax, az),
        P(ax + az, None),
        P(ax + az, None),
    )
    return jax.shard_map(
        local, mesh=fine, in_specs=placed, out_specs=P(ax + az, None), check_vma=False
    )
```
